32 devices in a mesh: rep: 1, cache: 32 (over z, y, x, core), owner: 1.
Axes of the slice: x: 2, y: 2, z: 4, core: 2. Of those that a mesh axis runs over, the one named last changes fastest.
Arguments:
- cache_rows: bfloat16 [65536, 128], P(('rep', 'cache')), may hold values from -1.796875 to 1.796875
- store_rows: bfloat16 [32768, 128], P(('rep', 'cache', 'owner')), may hold values from -1.796875 to 1.796875
- miss_block: int32 [32, 2], P(('rep', 'cache', 'owner')), may hold values from 0 to 7
- miss_slot: int32 [32, 2], P(('rep', 'cache')), may hold values from 0 to 16, as said below
- lookup_slot: int32 [32, 32, 624], P(('rep', 'cache', 'owner')), may hold values from 0 to 2047, as said below
- lookup_bag: int32 [32, 32, 624], P(('rep', 'cache', 'owner')), may hold values from 0 to 9984, as said below
- dense_rows: bfloat16 [12288, 128], P(('rep', 'cache', 'owner')), may hold values from -1.796875 to 1.796875
- w_first: bfloat16 [479, 2048], P(None, 'owner'), may hold values from -0.25 to 0.25
- w_second: bfloat16 [2048, 512], P('owner'), may hold values from -0.125 to 0.125
- w_out: float32 [512], replicated, may hold values from -0.25 to 0.25
Outputs:
- logits: float32 [12288], P(('rep', 'cache', 'owner'))
The draws below stay inside these ranges and needn't reach their ends.
Inputs may be any that keep to these rules, and one draw needn't show every extreme that they name: `miss_slot`: A value of 16 means no fill; the other values of a row are distinct; owner o's entries are o * 2 onward, used ones first, and in every row some owner uses all 2. `lookup_slot`: the cache slot map already applied: a local slot of cache shard d; 0 where the entry is empty. `lookup_bag`: 9984 marks an empty entry; in each bucket the used entries come first, and every device has a bucket with all 624 used.
All inputs are finite; a program needn't handle non-finite values.
Results may differ from the reference program's by a relative error of at most 0.006.
Values may be sent and summed in bfloat16 or wider, within the bound.
No kernel may reach another device: no remote copies, remote signals or barrier semaphores. Data moves between devices by JAX's collectives and lax.ppermute only.
A program may use at most 64 MiB of HBM per device.

```python
import jax
import jax.numpy as jnp
import numpy as np
from jax import lax

E = 128
F = 26
H = 2048
H2 = 512
BLOCK = 128
Q_DEV = 384
SLOTS = 2048
STORE_BLK = 8
MISS_CAP = 2
CACHE_SHARDS = 32
OWNERS = 1
SOURCES = 32
SLOT_BLKS = 16
BAGS = 9984
CAP = 624
INTER = 479
BATCH = 12288


def bucket_used(key):
    drawn = jax.random.randint(key, (SOURCES, CACHE_SHARDS), CAP // 2, CAP + 1)
    chosen = jnp.arange(SOURCES)[:, None] % CACHE_SHARDS == jnp.arange(CACHE_SHARDS)[None, :]
    drawn = jnp.where(chosen, CAP, drawn)
    return jnp.arange(CAP)[None, None, :] < drawn[:, :, None]


def draw_lookup_slot(key, part):
    in_use = bucket_used(key)
    key = jax.random.fold_in(key, 11)
    drawn = jax.random.randint(key, (SOURCES, CACHE_SHARDS, CAP), 0, SLOTS)
    return jnp.where(in_use, drawn, 0).astype(jnp.int32)


def draw_lookup_bag(key, part):
    in_use = bucket_used(key)
    key = jax.random.fold_in(key, 12)
    drawn = jax.random.randint(key, (SOURCES, CACHE_SHARDS, CAP), 0, BAGS)
    return jnp.where(in_use, drawn, BAGS).astype(jnp.int32)


def draw_miss_slot(key, part):
    key = jax.random.fold_in(key, 13)
    row_keys = jax.random.split(key, CACHE_SHARDS + 1)
    shuffled = jax.vmap(lambda one_key: jax.random.permutation(one_key, SLOT_BLKS))(row_keys[1:])
    shuffled = shuffled[:, :OWNERS * MISS_CAP]
    counts = jax.random.randint(row_keys[0], (CACHE_SHARDS, OWNERS), 1, MISS_CAP + 1)
    chosen = jnp.arange(CACHE_SHARDS)[:, None] % OWNERS == jnp.arange(OWNERS)[None, :]
    counts = jnp.where(chosen, MISS_CAP, counts)
    in_use = jnp.arange(MISS_CAP)[None, None, :] < counts[:, :, None]
    return jnp.where(in_use.reshape(CACHE_SHARDS, OWNERS * MISS_CAP), shuffled, SLOT_BLKS).astype(jnp.int32)


def touch_ends(entries, stream_key, low, largest):
    longest = entries.shape.index(max(entries.shape))
    spots = []
    for shift in (0, 1):
        where = [jax.random.randint(jax.random.fold_in(stream_key, axis), (), 0, length) for axis, length in enumerate(entries.shape)]
        where[longest] = (where[longest] + shift) % entries.shape[longest]
        spots.append(tuple(where))
    return entries.at[spots[0]].set(low).at[spots[1]].set(largest)


def steps_of(rng, dims, cuts, smallest, largest):
    loudness = 1.0
    for position, parts in cuts:
        steps = jax.random.uniform(jax.random.fold_in(jax.random.fold_in(rng, 6), position), (parts,), jnp.float32, smallest / len(cuts), largest / len(cuts))
        loudness = loudness * jnp.repeat(jnp.exp(steps), dims[position] // parts).reshape((-1,) + (1,) * (len(dims) - 1 - position))
    return loudness


def bell_draw(key, extent, spread, most, cuts=(), kind=jnp.bfloat16):
    values = spread * jax.random.normal(key, extent, jnp.float32)
    if cuts:
        values = values * steps_of(key, extent, cuts, -0.22, 0.18)
    return jnp.clip(values, -most, most).astype(kind)


def setup_inputs(seed: int = 0, part: int = 0) -> dict:
    key_of = jax.random.split(jax.random.key(seed), 11)
    part_splits = jax.random.split(jax.random.fold_in(key_of[10], part), 11)
    cache_rows = bell_draw(part_splits[0], (CACHE_SHARDS * SLOTS, E), 0.3, 1.796875, ((0, 32),))
    store_rows = bell_draw(part_splits[1], (SOURCES * STORE_BLK * BLOCK, E), 0.3, 1.796875, ((0, 32),))
    miss_block = touch_ends(jax.random.randint(part_splits[2], (SOURCES, MISS_CAP), 0, STORE_BLK), jax.random.fold_in(part_splits[2], 1), 0, STORE_BLK - 1).astype(jnp.int32)
    miss_slot = draw_miss_slot(jax.random.fold_in(jax.random.fold_in(key_of[10], part), 71), part)
    lookup_slot = draw_lookup_slot(jax.random.fold_in(jax.random.fold_in(key_of[10], part), 71), part)
    lookup_bag = draw_lookup_bag(jax.random.fold_in(jax.random.fold_in(key_of[10], part), 71), part)
    dense_rows = bell_draw(part_splits[6], (BATCH, E), 0.3, 1.796875, ((0, 32),))
    w_first = bell_draw(key_of[7], (INTER, H), INTER ** -0.5, 0.25)
    w_second = bell_draw(key_of[8], (H, H2), H ** -0.5, 0.125)
    w_out = bell_draw(key_of[9], (H2,), H2 ** -0.5, 0.25, (), jnp.float32)
    return {"cache_rows": cache_rows, "store_rows": store_rows, "miss_block": miss_block, "miss_slot": miss_slot, "lookup_slot": lookup_slot, "lookup_bag": lookup_bag, "dense_rows": dense_rows, "w_first": w_first, "w_second": w_second, "w_out": w_out}


def interact(dense_rows, pooled):
    stacked = jnp.concatenate([dense_rows[:, None, :], pooled], axis=1).astype(jnp.float32)
    products = jnp.einsum("qie,qje->qij", stacked, stacked, precision=lax.Precision.HIGHEST)
    upper_rows, upper_cols = np.triu_indices(F + 1, 1)
    paired = products[:, upper_rows, upper_cols].astype(jnp.bfloat16)
    return jnp.concatenate([dense_rows, paired], axis=1)


def head_layers(inter_in, w_first, w_second, w_out):
    hidden = jax.nn.relu(jnp.dot(inter_in, w_first, preferred_element_type=jnp.float32)).astype(jnp.bfloat16)
    second = jax.nn.relu(jnp.dot(hidden, w_second, preferred_element_type=jnp.float32))
    return jnp.sum(second * w_out, axis=1)


def reference(cache_rows, store_rows, miss_block, miss_slot, lookup_slot, lookup_bag, dense_rows, w_first, w_second, w_out):
    blocks = store_rows.reshape(SOURCES, STORE_BLK, BLOCK, E)
    picked = jax.vmap(lambda store_part, wanted: store_part[wanted])(blocks, miss_block)
    picked = picked.reshape(CACHE_SHARDS, OWNERS * MISS_CAP, BLOCK, E)
    cache_now = cache_rows.reshape(CACHE_SHARDS, SLOT_BLKS, BLOCK, E)
    filled_cache = jax.vmap(lambda shard_rows, slot_ids, new_rows: shard_rows.at[slot_ids].set(new_rows, mode="drop"))(cache_now, miss_slot, picked)
    filled_cache = filled_cache.reshape(CACHE_SHARDS, SLOTS, E)
    shard_ids = jnp.arange(CACHE_SHARDS, dtype=jnp.int32)[:, None]

    def one_source(source_args):
        slot_ids, bag_ids, own_dense = source_args
        arrived = filled_cache[shard_ids, slot_ids]
        pooled = jax.ops.segment_sum(arrived.reshape(-1, E).astype(jnp.float32), bag_ids.reshape(-1), num_segments=BAGS, mode="drop")
        pooled = pooled.astype(jnp.bfloat16).reshape(Q_DEV, F, E)
        return head_layers(interact(own_dense, pooled), w_first, w_second, w_out)

    logits = lax.map(one_source, (lookup_slot, lookup_bag, dense_rows.reshape(SOURCES, Q_DEV, E)))
    return logits.reshape(-1)
```

```python
import functools

import jax
import jax.numpy as jnp
from jax import lax
from jax.experimental import pallas as pl
from jax.experimental.pallas import tpu as pltpu
from jax.sharding import PartitionSpec as P

F = 26
BLOCK = 128
VECS = F + 1
LANES = 128
CHAINS = 4
UNROLL = 8
VMEM = 56 << 20


def fill_kernel(slot_ref, block_ref, cache_ref, fills_ref, out_ref, sem):
    def of_block(ref, index):
        return ref.at[pl.ds(pl.multiple_of(index * BLOCK, BLOCK), BLOCK)]

    n_slots = out_ref.shape[0] // BLOCK
    n_fills = slot_ref.shape[0]

    def kept(index):
        hit = slot_ref[0] == index
        for k in range(1, n_fills):
            hit = jnp.logical_or(hit, slot_ref[k] == index)
        return jnp.logical_not(hit)

    def cache_copy(index):
        return pltpu.make_async_copy(of_block(cache_ref, index), of_block(out_ref, index), sem.at[index])

    def fill_copy(k):
        slot = jnp.minimum(slot_ref[k], n_slots - 1)
        return pltpu.make_async_copy(
            of_block(fills_ref, block_ref[k]), of_block(out_ref, slot), sem.at[n_slots + k]
        )

    for index in range(n_slots):
        pl.when(kept(index))(lambda index=index: cache_copy(index).start())
    for k in range(n_fills):
        pl.when(slot_ref[k] < n_slots)(lambda k=k: fill_copy(k).start())
    for index in range(n_slots):
        pl.when(kept(index))(lambda index=index: cache_copy(index).wait())
    for k in range(n_fills):
        pl.when(slot_ref[k] < n_slots)(lambda k=k: fill_copy(k).wait())


def fill(cache_rows, fills, miss_slot, fill_block):
    n_sems = cache_rows.shape[0] // BLOCK + miss_slot.shape[0]
    return pl.pallas_call(
        fill_kernel,
        out_shape=jax.ShapeDtypeStruct(cache_rows.shape, cache_rows.dtype),
        in_specs=[pl.BlockSpec(memory_space=pltpu.SMEM)] * 2 + [pl.BlockSpec(memory_space=pl.ANY)] * 2,
        out_specs=pl.BlockSpec(memory_space=pl.ANY),
        scratch_shapes=[pltpu.SemaphoreType.DMA((n_sems,))],
        name="fill",
    )(miss_slot, fill_block, cache_rows, fills)


def pool_shards(slot_ref, bag_ref, count_ref, shards, sems, held, table, sums, cap):
    copies = [pltpu.make_async_copy(ref, held.at[s], sems.at[s]) for s, ref in enumerate(shards)]
    for copy in copies:
        copy.start()
    yield
    for s, copy in enumerate(copies):
        copy.wait()
        table[...] = held[s].astype(jnp.float32)

        def add_entries(step, _):
            first = s * cap + step * UNROLL
            for group in range(UNROLL // CHAINS):
                entries = [first + group * CHAINS + k for k in range(CHAINS)]
                slots = [slot_ref[e] for e in entries]
                bags = [bag_ref[e] for e in entries]
                rows = [table[pl.ds(slot, 1), :] for slot in slots]
                olds = [sums[k][pl.ds(bags[k], 1), :] for k in range(CHAINS)]
                for k in range(CHAINS):
                    sums[k][pl.ds(bags[k], 1), :] = olds[k] + rows[k]
            return 0

        lax.fori_loop(0, count_ref[s], add_entries, 0)


def start_sums(sums, total_ref, sem):
    if total_ref is None:
        sums[0][...] = jnp.zeros_like(sums[0])
    else:
        pltpu.make_async_copy(total_ref, sums[0], sem).start()
    for one in sums[1:]:
        one[...] = jnp.zeros_like(one)
    if total_ref is not None:
        pltpu.make_async_copy(total_ref, sums[0], sem).wait()


def pool_kernel(n_shards, has_total, cap, slot_ref, bag_ref, count_ref, *refs):
    shards, refs = refs[:n_shards], refs[n_shards:]
    total_in, refs = (refs[0], refs[1:]) if has_total else (None, refs)
    total_out, held, table, *sums, sems, total_sem = refs
    pooling = pool_shards(slot_ref, bag_ref, count_ref, shards, sems, held, table, sums, cap)
    next(pooling)
    start_sums(sums, total_in, total_sem)
    for _ in pooling:
        pass
    rows = sums[0].shape[0]
    step = LANES
    n_steps = rows // step

    def add_up(index, _):
        part = pl.ds(pl.multiple_of(index * step, 8), step)
        total = sums[0][part, :]
        for one in sums[1:]:
            total = total + one[part, :]
        sums[0][part, :] = total
        return 0

    lax.fori_loop(0, n_steps, add_up, 0)
    copy = pltpu.make_async_copy(sums[0], total_out, total_sem)
    copy.start()
    copy.wait()


def interact(sums, dense_ref, masked, queries):
    lane = lax.broadcasted_iota(jnp.int32, (8, 256), 1)
    row = lax.broadcasted_iota(jnp.int32, (8, 256), 0)
    own_query = (lane & 7) == row

    def sixteen_queries(step, _):
        dense = dense_ref[pl.ds(pl.multiple_of(step * 16, 16), 16), :].astype(jnp.float32)
        halves = []
        for half in range(2):
            query = pl.multiple_of(step * 16 + half * 8, 8)
            vectors = [dense[half * 8 : half * 8 + 8]]
            for feature in range(F):
                rows = pl.ds(pl.multiple_of(feature * queries + query, 8), 8)
                total = sums[0][rows, :]
                for one in sums[1:]:
                    total = total + one[rows, :]
                vectors.append(total)
            vectors += [jnp.zeros((8, LANES), jnp.float32)] * (32 - VECS)
            stacked = jnp.concatenate(vectors, axis=0).astype(jnp.bfloat16)
            halves.append(
                lax.dot_general(
                    stacked, stacked, (((1,), (1,)), ((), ())), preferred_element_type=jnp.float32
                )
            )
        for i in range(F):
            pair = [
                jnp.where(own_query, products[8 * i : 8 * i + 8, :], 0.0) for products in halves
            ]
            masked[i, pl.ds(pl.multiple_of(step * 16, 16), 16), :] = jnp.concatenate(
                pair, axis=0
            ).astype(jnp.bfloat16)
        return 0

    lax.fori_loop(0, queries // 16, sixteen_queries, 0)


def inter_columns(masked, dense_ref, inter, queries):
    spread = lax.broadcasted_iota(jnp.int32, (256, LANES), 0) // 8
    vector = lax.broadcasted_iota(jnp.int32, (256, LANES), 1)
    pick = jnp.where(spread == vector, 1.0, 0.0).astype(jnp.bfloat16)
    lane = lax.broadcasted_iota(jnp.int32, (queries, LANES), 1)
    tiles = [jnp.zeros((queries, LANES), jnp.float32) for _ in range(3)]
    first = 0
    for i in range(F):
        length = F - i
        picked = jnp.dot(masked[i], pick, preferred_element_type=jnp.float32)
        shift = (first - (i + 1)) % LANES
        if shift:
            picked = pltpu.roll(picked, shift, 1)
        for tile in range(3):
            low, high = max(first, tile * LANES), min(first + length, (tile + 1) * LANES)
            if low < high:
                inside = jnp.logical_and(lane >= low - tile * LANES, lane < high - tile * LANES)
                tiles[tile] = jnp.where(inside, picked, tiles[tile])
        first += length
    inter[:, :LANES] = dense_ref[...]
    for tile in range(3):
        inter[:, (tile + 1) * LANES : (tile + 2) * LANES] = tiles[tile].astype(jnp.bfloat16)


def final_kernel(n_shards, cap, with_head, slot_ref, bag_ref, count_ref, *refs):
    shards, refs = refs[:n_shards], refs[n_shards:]
    total_in, dense_ref, refs = refs[0], refs[1], refs[2:]
    if with_head:
        w_first, w_second, w_out, logits, inter, masked, first_held, second_held, weight_sems, *refs = refs
        weights = [
            pltpu.make_async_copy(w_first, first_held, weight_sems.at[0]),
            pltpu.make_async_copy(w_second, second_held, weight_sems.at[1]),
        ]
        for copy in weights:
            copy.start()
    else:
        inter, masked, *refs = refs
    held, table, *sums, sems, total_sem = refs
    queries = dense_ref.shape[0]
    pooling = pool_shards(slot_ref, bag_ref, count_ref, shards, sems, held, table, sums, cap)
    next(pooling)
    start_sums(sums, total_in, total_sem)
    for _ in pooling:
        pass
    interact(sums, dense_ref, masked, queries)
    inter_columns(masked, dense_ref, inter, queries)
    if not with_head:
        return
    for copy in weights:
        copy.wait()
    step = LANES
    for part in range(queries // step):
        rows = slice(part * step, (part + 1) * step)
        hidden = jnp.dot(inter[rows, :], first_held[...], preferred_element_type=jnp.float32)
        hidden = jnp.maximum(hidden, 0.0).astype(jnp.bfloat16)
        second = jnp.dot(hidden, second_held[...], preferred_element_type=jnp.float32)
        scored = jnp.maximum(second, 0.0) * w_out[...]
        folded = scored[:, :LANES]
        for tile in range(1, scored.shape[1] // LANES):
            folded = folded + scored[:, tile * LANES : (tile + 1) * LANES]
        logits[:, rows] = jnp.sum(folded.T, axis=0, keepdims=True)


def pool_scratch(n_shards, shard_rows, sum_rows):
    return (
        [pltpu.VMEM((n_shards, shard_rows, LANES), jnp.bfloat16), pltpu.VMEM((shard_rows, LANES), jnp.float32)]
        + [pltpu.VMEM((sum_rows, LANES), jnp.float32)] * CHAINS
        + [pltpu.SemaphoreType.DMA((n_shards,)), pltpu.SemaphoreType.DMA]
    )


SMEM_SPEC = pl.BlockSpec(memory_space=pltpu.SMEM)
ANY_SPEC = pl.BlockSpec(memory_space=pl.ANY)
VMEM_SPEC = pl.BlockSpec(memory_space=pltpu.VMEM)


def pool(slots, bags, counts, shards, total, cap, sum_rows):
    n_shards = len(shards)
    totals = [] if total is None else [total]
    return pl.pallas_call(
        functools.partial(pool_kernel, n_shards, total is not None, cap),
        out_shape=jax.ShapeDtypeStruct((sum_rows, LANES), jnp.float32),
        in_specs=[SMEM_SPEC] * 3 + [ANY_SPEC] * (n_shards + len(totals)),
        out_specs=ANY_SPEC,
        scratch_shapes=pool_scratch(n_shards, shards[0].shape[0], sum_rows),
        compiler_params=pltpu.CompilerParams(vmem_limit_bytes=VMEM),
        cost_estimate=pl.CostEstimate(flops=0, bytes_accessed=n_shards * 4_000_000, transcendentals=0),
        name="pool",
    )(slots, bags, counts, *shards, *totals)


def finish(slots, bags, counts, shards, total, cap, sum_rows, dense_rows, head):
    n_shards = len(shards)
    queries = dense_rows.shape[0]
    width = 4 * LANES
    masked = pltpu.VMEM((F, queries, 256), jnp.bfloat16)
    if head is None:
        head_args, head_specs = [], []
        out_shape = jax.ShapeDtypeStruct((queries, width), jnp.bfloat16)
        scratch = [masked]
    else:
        head_args, head_specs = list(head), [ANY_SPEC, ANY_SPEC, VMEM_SPEC]
        out_shape = jax.ShapeDtypeStruct((1, queries), jnp.float32)
        scratch = [
            pltpu.VMEM((queries, width), jnp.bfloat16),
            masked,
            pltpu.VMEM(head[0].shape, jnp.bfloat16),
            pltpu.VMEM(head[1].shape, jnp.bfloat16),
            pltpu.SemaphoreType.DMA((2,)),
        ]
    return pl.pallas_call(
        functools.partial(final_kernel, n_shards, cap, head is not None),
        out_shape=out_shape,
        in_specs=[SMEM_SPEC] * 3 + [ANY_SPEC] * (n_shards + 1) + [VMEM_SPEC] + head_specs,
        out_specs=VMEM_SPEC,
        scratch_shapes=scratch + pool_scratch(n_shards, shards[0].shape[0], sum_rows),
        compiler_params=pltpu.CompilerParams(vmem_limit_bytes=VMEM),
        name="finish",
    )(slots, bags, counts, *shards, total, dense_rows, *head_args)


def per_device(
    n_planes,
    cache_rows,
    store_rows,
    miss_block,
    miss_slot,
    lookup_slot,
    lookup_bag,
    dense_rows,
    w_first,
    w_second,
    w_out,
):
    emb_width = cache_rows.shape[1]
    queries = dense_rows.shape[0]
    bags = queries * F
    owners = lax.axis_size("owner")
    n_shards = n_planes * 8

    if owners == 1:
        fills, fill_block = store_rows, miss_block[0]
    else:
        fills = store_rows.reshape(-1, BLOCK, emb_width)[miss_block[0]]
        fills = lax.all_gather(fills, "owner", axis=0, tiled=True)
        fill_block = jnp.arange(fills.shape[0], dtype=jnp.int32)
        fills = fills.reshape(-1, emb_width)
    own = fill(cache_rows, fills, miss_slot[0], fill_block)

    def device(z, y, x, core):
        return ((z * 2 + y) * 2 + x) * 2 + core

    def hop(move):
        pairs = []
        for index in range(n_shards):
            at = (index // 8, index // 4 % 2, index // 2 % 2, index % 2)
            pairs.append((index, device(*move(*at))))
        return lambda array: lax.ppermute(array, "cache", pairs)

    next_plane = hop(lambda z, y, x, core: ((z + 1) % n_planes, y, x, core))
    first_hop = hop(lambda z, y, x, core: (z, y, 1 - x, core) if core == 0 else (z, 1 - y, x, core))
    second_hop = hop(lambda z, y, x, core: (z, 1 - y, x, core) if core == 0 else (z, y, 1 - x, core))
    other_core = hop(lambda z, y, x, core: (z, y, x, 1 - core))

    me = lax.axis_index("cache")
    z, y, x, core = me // 8, me // 4 % 2, me // 2 % 2, me % 2
    planes, order = [], []
    piece = own
    for shift in range(n_planes):
        if shift:
            piece = next_plane(piece)
        crossed = first_hop(piece)
        mine = [piece, crossed, second_hop(piece), second_hop(crossed)]
        planes.append(mine + [other_core(one) for one in mine])
        for side in (core, 1 - core):
            from_z = (z - shift) % n_planes
            for flip_first, flip_second in ((0, 0), (1, 0), (0, 1), (1, 1)):
                flip_x = jnp.where(side == 0, flip_first, flip_second)
                flip_y = jnp.where(side == 0, flip_second, flip_first)
                order.append(device(from_z, y ^ flip_y, x ^ flip_x, side))
    order = jnp.stack(order)

    cap = lookup_slot.shape[2]
    cap += -cap % UNROLL
    spare = ((0, 0), (0, cap - lookup_slot.shape[2]))
    slots = jnp.pad(lookup_slot[0], spare)[order]
    bag_ids = jnp.pad(lookup_bag[0], spare, constant_values=bags)[order]
    used = jnp.sum((bag_ids < bags).astype(jnp.int32), axis=1)
    steps = (used + UNROLL - 1) // UNROLL
    sum_rows = bags + 8
    places = jnp.where(bag_ids < bags, bag_ids % F * queries + bag_ids // F, bags)

    groups = [list(range(n_planes - 2))[: n_planes // 2]]
    groups += [[plane] for plane in range(len(groups[0]), n_planes)]
    total = None
    for group in groups:
        part = slice(8 * group[0], 8 * group[-1] + 8)
        args = (slots[part].reshape(-1), places[part].reshape(-1), steps[part])
        shards = [one for plane in group for one in planes[plane]]
        if group is not groups[-1]:
            total = pool(*args, shards, total, cap, sum_rows)
    short = -w_first.shape[0] % LANES
    w_first = jnp.pad(w_first, ((0, short), (0, 0)))
    if owners == 1:
        head = (w_first, w_second, w_out.reshape(1, -1))
        logits = finish(*args, shards, total, cap, sum_rows, dense_rows, head)
        return logits.reshape(-1)
    inter_in = finish(*args, shards, total, cap, sum_rows, dense_rows, None)
    group_inputs = lax.all_gather(inter_in, "owner", axis=0, tiled=True)
    hidden = jax.nn.relu(jnp.dot(group_inputs, w_first, preferred_element_type=jnp.float32))
    second = lax.psum_scatter(
        jnp.dot(hidden.astype(jnp.bfloat16), w_second, preferred_element_type=jnp.float32),
        "owner",
        scatter_dimension=0,
        tiled=True,
    )
    return jnp.sum(jax.nn.relu(second) * w_out, axis=1)


def solution(mesh):
    in_specs = (
        P(("rep", "cache"), None),
        P(("rep", "cache", "owner"), None),
        P(("rep", "cache", "owner"), None),
        P(("rep", "cache"), None),
        P(("rep", "cache", "owner"), None, None),
        P(("rep", "cache", "owner"), None, None),
        P(("rep", "cache", "owner"), None),
        P(None, "owner"),
        P("owner", None),
        P(),
    )
    out_specs = P(("rep", "cache", "owner"))
    return jax.shard_map(
        functools.partial(per_device, mesh.shape["cache"] // 8),
        mesh=mesh,
        in_specs=in_specs,
        out_specs=out_specs,
        check_vma=False,
    )
```

```python
import functools

import jax
import jax.numpy as jnp
from jax import lax
from jax.experimental import pallas as pl
from jax.experimental.pallas import tpu as pltpu
from jax.sharding import PartitionSpec as P

F = 26
BLOCK = 128
VECS = F + 1
LANES = 128
CHAINS = 4
UNROLL = 8
VMEM = 32 << 20
SMEM_SPEC = pl.BlockSpec(memory_space=pltpu.SMEM)
ANY_SPEC = pl.BlockSpec(memory_space=pl.ANY)
HBM_SPEC = pl.BlockSpec(memory_space=pltpu.HBM)
VMEM_SPEC = pl.BlockSpec(memory_space=pltpu.VMEM)


def fill_kernel(slot_ref, block_ref, cache_ref, fills_ref, out_ref, sem):
    def of_block(ref, index):
        return ref.at[pl.ds(pl.multiple_of(index * BLOCK, BLOCK), BLOCK)]

    n_slots = out_ref.shape[0] // BLOCK
    n_fills = slot_ref.shape[0]

    def kept(index):
        hit = slot_ref[0] == index
        for k in range(1, n_fills):
            hit = jnp.logical_or(hit, slot_ref[k] == index)
        return jnp.logical_not(hit)

    def cache_copy(index):
        return pltpu.make_async_copy(of_block(cache_ref, index), of_block(out_ref, index), sem.at[index])

    def fill_copy(k):
        slot = jnp.minimum(slot_ref[k], n_slots - 1)
        return pltpu.make_async_copy(
            of_block(fills_ref, block_ref[k]), of_block(out_ref, slot), sem.at[n_slots + k]
        )

    for k in range(n_fills):
        pl.when(slot_ref[k] < n_slots)(lambda k=k: fill_copy(k).start())
    for index in range(n_slots):
        pl.when(kept(index))(lambda index=index: cache_copy(index).start())
    for index in range(n_slots):
        pl.when(kept(index))(lambda index=index: cache_copy(index).wait())
    for k in range(n_fills):
        pl.when(slot_ref[k] < n_slots)(lambda k=k: fill_copy(k).wait())


def fill(cache_rows, fills, miss_slot, fill_block):
    n_sems = cache_rows.shape[0] // BLOCK + miss_slot.shape[0]
    return pl.pallas_call(
        fill_kernel,
        out_shape=jax.ShapeDtypeStruct(cache_rows.shape, cache_rows.dtype),
        in_specs=[SMEM_SPEC] * 2 + [ANY_SPEC] * 2,
        out_specs=VMEM_SPEC,
        scratch_shapes=[pltpu.SemaphoreType.DMA((n_sems,))],
        name="fill",
    )(miss_slot, fill_block, cache_rows, fills)


def gate_kernel(*refs):
    pass


def gate(arrays, after):
    n_arrays = len(arrays)
    return pl.pallas_call(
        gate_kernel,
        out_shape=[jax.ShapeDtypeStruct(one.shape, one.dtype) for one in arrays],
        in_specs=[HBM_SPEC] * n_arrays + [SMEM_SPEC],
        out_specs=[HBM_SPEC] * n_arrays,
        input_output_aliases={index: index for index in range(n_arrays)},
        compiler_params=pltpu.CompilerParams(vmem_limit_bytes=1 << 20),
        name="gate",
    )(*arrays, after)


def pool_shards(first, entry_refs, entry_held, count_ref, shards, sems, held, table, sums):
    copies = [
        pltpu.make_async_copy(ref.at[pl.ds(first, 8)], to, sems.at[len(shards) + index])
        for index, (ref, to) in enumerate(zip(entry_refs, entry_held))
    ]
    copies += [pltpu.make_async_copy(ref, held.at[s], sems.at[s]) for s, ref in enumerate(shards)]
    for copy in copies:
        copy.start()
    yield
    for copy in copies[:2]:
        copy.wait()
    slot_ref, bag_ref = entry_held
    skipped = 2 if first == 0 else 0
    for s, copy in enumerate(copies[2:]):
        copy.wait()
        table[...] = held[s].astype(jnp.float32)
        row = s + skipped

        def add_entries(step, _):
            first = step * UNROLL
            for group in range(UNROLL // CHAINS):
                entries = [first + group * CHAINS + k for k in range(CHAINS)]
                slots = [slot_ref[row, e] for e in entries]
                bags = [bag_ref[row, e] for e in entries]
                rows = [table[pl.ds(slot, 1), :] for slot in slots]
                olds = [sums[k][pl.ds(bags[k], 1), :] for k in range(CHAINS)]
                for k in range(CHAINS):
                    sums[k][pl.ds(bags[k], 1), :] = olds[k] + rows[k]
            return 0

        lax.fori_loop(0, count_ref[first + row], add_entries, 0)


def pool_kernel(first, n_shards, is_first, count_ref, slot_ref, bag_ref, *refs):
    shards, refs = refs[:n_shards], refs[n_shards:]
    if not is_first:
        refs = refs[CHAINS:]
    sums, (done, *entry_held, held, table, sems) = refs[:CHAINS], refs[CHAINS:]
    pooling = pool_shards(
        first, (slot_ref, bag_ref), entry_held, count_ref, shards, sems, held, table, sums
    )
    next(pooling)
    if is_first:
        for one in sums:
            one[...] = jnp.zeros_like(one)
    for _ in pooling:
        pass
    done[0] = 0


def interact(sums, dense_ref, masked, queries):
    lane = lax.broadcasted_iota(jnp.int32, (8, 256), 1)
    row = lax.broadcasted_iota(jnp.int32, (8, 256), 0)
    own_query = (lane & 7) == row

    def sixteen_queries(step, _):
        dense = dense_ref[pl.ds(pl.multiple_of(step * 16, 16), 16), :].astype(jnp.float32)
        halves = []
        for half in range(2):
            query = pl.multiple_of(step * 16 + half * 8, 8)
            vectors = [dense[half * 8 : half * 8 + 8]]
            for feature in range(F):
                rows = pl.ds(pl.multiple_of(feature * queries + query, 8), 8)
                total = sums[0][rows, :]
                for one in sums[1:]:
                    total = total + one[rows, :]
                vectors.append(total)
            vectors += [jnp.zeros((8, LANES), jnp.float32)] * (32 - VECS)
            stacked = jnp.concatenate(vectors, axis=0).astype(jnp.bfloat16)
            halves.append(
                lax.dot_general(
                    stacked, stacked, (((1,), (1,)), ((), ())), preferred_element_type=jnp.float32
                )
            )
        for i in range(F):
            pair = [
                jnp.where(own_query, products[8 * i : 8 * i + 8, :], 0.0) for products in halves
            ]
            masked[i, pl.ds(pl.multiple_of(step * 16, 16), 16), :] = jnp.concatenate(
                pair, axis=0
            ).astype(jnp.bfloat16)
        return 0

    lax.fori_loop(0, queries // 16, sixteen_queries, 0)


def inter_columns(masked, dense_ref, inter, queries):
    spread = lax.broadcasted_iota(jnp.int32, (256, LANES), 0) // 8
    vector = lax.broadcasted_iota(jnp.int32, (256, LANES), 1)
    pick = jnp.where(spread == vector, 1.0, 0.0).astype(jnp.bfloat16)
    lane = lax.broadcasted_iota(jnp.int32, (queries, LANES), 1)
    tiles = [jnp.zeros((queries, LANES), jnp.float32) for _ in range(3)]
    first = 0
    for i in range(F):
        length = F - i
        picked = jnp.dot(masked[i], pick, preferred_element_type=jnp.float32)
        shift = (first - (i + 1)) % LANES
        if shift:
            picked = pltpu.roll(picked, shift, 1)
        for tile in range(3):
            low, high = max(first, tile * LANES), min(first + length, (tile + 1) * LANES)
            if low < high:
                inside = jnp.logical_and(lane >= low - tile * LANES, lane < high - tile * LANES)
                tiles[tile] = jnp.where(inside, picked, tiles[tile])
        first += length
    inter[:, :LANES] = dense_ref[...]
    for tile in range(3):
        inter[:, (tile + 1) * LANES : (tile + 2) * LANES] = tiles[tile].astype(jnp.bfloat16)


def final_kernel(first, n_shards, with_head, count_ref, slot_ref, bag_ref, *refs):
    shards, refs = refs[:n_shards], refs[n_shards:]
    old_sums, dense_ref, refs = refs[:CHAINS], refs[CHAINS], refs[CHAINS + 1 :]
    if with_head:
        w_first, w_second, w_out, logits, *refs = refs
    else:
        inter, *refs = refs
    refs = refs[CHAINS:]
    if with_head:
        inter, first_held, second_held, weight_sems, *refs = refs
        weights = [
            pltpu.make_async_copy(w_first, first_held, weight_sems.at[0]),
            pltpu.make_async_copy(w_second, second_held, weight_sems.at[1]),
        ]
        for copy in weights:
            copy.start()
    masked, *entry_held, held, table, sems = refs
    queries = dense_ref.shape[0]
    for _ in pool_shards(
        first, (slot_ref, bag_ref), entry_held, count_ref, shards, sems, held, table, old_sums
    ):
        pass
    interact(old_sums, dense_ref, masked, queries)
    inter_columns(masked, dense_ref, inter, queries)
    if not with_head:
        return
    for copy in weights:
        copy.wait()
    step = LANES
    inputs = first_held.shape[0]
    for part in range(queries // step):
        rows = slice(part * step, (part + 1) * step)
        hidden = jnp.dot(inter[rows, :inputs], first_held[...], preferred_element_type=jnp.float32)
        hidden = jnp.maximum(hidden, 0.0).astype(jnp.bfloat16)
        second = jnp.dot(hidden, second_held[...], preferred_element_type=jnp.float32)
        scored = jnp.maximum(second, 0.0) * w_out[...]
        folded = scored[:, :LANES]
        for tile in range(1, scored.shape[1] // LANES):
            folded = folded + scored[:, tile * LANES : (tile + 1) * LANES]
        logits[rows] = jnp.sum(folded.T, axis=0)


def pool_scratch(n_shards, shard_rows, cap):
    return [
        pltpu.SMEM((8, cap), jnp.int32),
        pltpu.SMEM((8, cap), jnp.int32),
        pltpu.VMEM((n_shards, shard_rows, LANES), jnp.bfloat16),
        pltpu.VMEM((shard_rows, LANES), jnp.float32),
        pltpu.SemaphoreType.DMA((n_shards + 2,)),
    ]


def pool(first, entries, shards, sums, sum_rows):
    n_shards = len(shards)
    is_first = sums is None
    sums = [] if is_first else sums
    *sums, done = pl.pallas_call(
        functools.partial(pool_kernel, first, n_shards, is_first),
        out_shape=[pltpu.VMEM((sum_rows, LANES), jnp.float32)] * CHAINS
        + [jax.ShapeDtypeStruct((1,), jnp.int32)],
        in_specs=[SMEM_SPEC] + [HBM_SPEC] * (2 + n_shards) + [VMEM_SPEC] * len(sums),
        out_specs=[VMEM_SPEC] * CHAINS + [SMEM_SPEC],
        input_output_aliases={3 + n_shards + k: k for k in range(len(sums))},
        scratch_shapes=pool_scratch(n_shards, shards[0].shape[0], entries[1].shape[1]),
        compiler_params=pltpu.CompilerParams(vmem_limit_bytes=VMEM),
        cost_estimate=pl.CostEstimate(flops=0, bytes_accessed=n_shards * 6_000_000, transcendentals=0),
        name="pool",
    )(*entries, *shards, *sums)
    return sums, done


def finish(first, entries, shards, sums, dense_rows, head):
    n_shards = len(shards)
    queries = dense_rows.shape[0]
    width = 4 * LANES
    masked = pltpu.VMEM((F, queries, 256), jnp.bfloat16)
    if head is None:
        head_args, head_specs = [], []
        out_shape = jax.ShapeDtypeStruct((queries, width), jnp.bfloat16)
        scratch = [masked]
    else:
        head_args, head_specs = list(head), [HBM_SPEC, HBM_SPEC, VMEM_SPEC]
        out_shape = jax.ShapeDtypeStruct((queries,), jnp.float32)
        scratch = [
            pltpu.VMEM((queries, width), jnp.bfloat16),
            pltpu.VMEM(head[0].shape, jnp.bfloat16),
            pltpu.VMEM(head[1].shape, jnp.bfloat16),
            pltpu.SemaphoreType.DMA((2,)),
            masked,
        ]
    out = pl.pallas_call(
        functools.partial(final_kernel, first, n_shards, head is not None),
        out_shape=[out_shape] + [pltpu.VMEM(one.shape, one.dtype) for one in sums],
        in_specs=[SMEM_SPEC] + [HBM_SPEC] * (2 + n_shards) + [VMEM_SPEC] * (CHAINS + 1) + head_specs,
        out_specs=[VMEM_SPEC] * (CHAINS + 1),
        input_output_aliases={3 + n_shards + k: 1 + k for k in range(CHAINS)},
        scratch_shapes=scratch + pool_scratch(n_shards, shards[0].shape[0], entries[1].shape[1]),
        compiler_params=pltpu.CompilerParams(vmem_limit_bytes=VMEM),
        name="finish",
    )(*entries, *shards, *sums, dense_rows, *head_args)
    return out[0]


def per_device(
    n_planes,
    cache_rows,
    store_rows,
    miss_block,
    miss_slot,
    lookup_slot,
    lookup_bag,
    dense_rows,
    w_first,
    w_second,
    w_out,
):
    emb_width = cache_rows.shape[1]
    queries = dense_rows.shape[0]
    bags = queries * F
    owners = lax.axis_size("owner")
    n_shards = n_planes * 8

    if owners == 1:
        fills, fill_block = store_rows, miss_block[0]
    else:
        fills = store_rows.reshape(-1, BLOCK, emb_width)[miss_block[0]]
        fills = lax.all_gather(fills, "owner", axis=0, tiled=True)
        fill_block = jnp.arange(fills.shape[0], dtype=jnp.int32)
        fills = fills.reshape(-1, emb_width)
    own = fill(cache_rows, fills, miss_slot[0], fill_block)

    def device(z, y, x, core):
        return ((z * 2 + y) * 2 + x) * 2 + core

    def hop(move):
        pairs = []
        for index in range(n_shards):
            at = (index // 8, index // 4 % 2, index // 2 % 2, index % 2)
            pairs.append((index, device(*move(*at))))
        return lambda array: lax.ppermute(array, "cache", pairs)

    next_plane = hop(lambda z, y, x, core: ((z + 1) % n_planes, y, x, core))
    first_hop = hop(lambda z, y, x, core: (z, y, 1 - x, core) if core == 0 else (z, 1 - y, x, core))
    second_hop = hop(lambda z, y, x, core: (z, 1 - y, x, core) if core == 0 else (z, y, 1 - x, core))
    other_core = hop(lambda z, y, x, core: (z, y, x, 1 - core))

    me = lax.axis_index("cache")
    z, y, x, core = me // 8, me // 4 % 2, me // 2 % 2, me % 2

    def origin(shift, flip_first, flip_second, side):
        flip_x = jnp.where(side == 0, flip_first, flip_second)
        flip_y = jnp.where(side == 0, flip_second, flip_first)
        return device((z - shift) % n_planes, y ^ flip_y, x ^ flip_x, side)

    def both_cores(shift, *flips):
        return [origin(shift, *flips, side) for side in (core, 1 - core)]

    order = []
    for shift in range(n_planes + 1):
        before, now = max(shift - 1, 0), min(shift, n_planes - 1)
        order += both_cores(before, 1, 1)
        for flips in ((0, 0), (1, 0), (0, 1)):
            order += both_cores(now, *flips)
    order = jnp.stack(order)
    cap = lookup_slot.shape[2]
    cap += -cap % UNROLL
    spare = ((0, 0), (0, cap - lookup_slot.shape[2]))
    slots = jnp.pad(lookup_slot[0], spare)[order]
    bag_ids = jnp.pad(lookup_bag[0], spare, constant_values=bags)[order]
    used = jnp.sum((bag_ids < bags).astype(jnp.int32), axis=1)
    steps = (used + UNROLL - 1) // UNROLL
    sum_rows = bags + 8
    places = jnp.where(bag_ids < bags, bag_ids % F * queries + bag_ids // F, bags)
    entries = (steps, slots, places)

    sums, far = None, []
    piece, crossed, turned = own, first_hop(own), second_hop(own)
    next_piece = next_plane(piece)
    for shift in range(n_planes):
        near = [piece, other_core(piece), crossed, other_core(crossed), turned, other_core(turned)]
        next_far = second_hop(crossed)
        if shift < n_planes - 1:
            next_crossed, next_turned = first_hop(next_piece), second_hop(next_piece)
            passed = [next_piece, next_crossed, next_turned]
            if shift < n_planes - 2:
                passed.append(next_plane(next_piece))
        sums, done = pool(8 * shift, entries, far + near, sums, sum_rows)
        if shift < n_planes - 1:
            next_far, piece, crossed, turned, *next_piece = gate([next_far] + passed, done)
            next_piece = next_piece[0] if next_piece else None
        far = [next_far, other_core(next_far)]
    args = (8 * n_planes, entries, far, sums, dense_rows)
    if owners == 1:
        return finish(*args, (w_first, w_second, w_out.reshape(1, -1)))
    inter_in = finish(*args, None)[:, : w_first.shape[0]]
    group_inputs = lax.all_gather(inter_in, "owner", axis=0, tiled=True)
    hidden = jax.nn.relu(jnp.dot(group_inputs, w_first, preferred_element_type=jnp.float32))
    second = lax.psum_scatter(
        jnp.dot(hidden.astype(jnp.bfloat16), w_second, preferred_element_type=jnp.float32),
        "owner",
        scatter_dimension=0,
        tiled=True,
    )
    return jnp.sum(jax.nn.relu(second) * w_out, axis=1)


def solution(mesh):
    in_specs = (
        P(("rep", "cache"), None),
        P(("rep", "cache", "owner"), None),
        P(("rep", "cache", "owner"), None),
        P(("rep", "cache"), None),
        P(("rep", "cache", "owner"), None, None),
        P(("rep", "cache", "owner"), None, None),
        P(("rep", "cache", "owner"), None),
        P(None, "owner"),
        P("owner", None),
        P(),
    )
    out_specs = P(("rep", "cache", "owner"))
    return jax.shard_map(
        functools.partial(per_device, mesh.shape["cache"] // 8),
        mesh=mesh,
        in_specs=in_specs,
        out_specs=out_specs,
        check_vma=False,
    )
```

```python
import functools

import jax
import jax.numpy as jnp
from jax import lax
from jax.experimental import pallas as pl
from jax.experimental.pallas import tpu as pltpu
from jax.sharding import PartitionSpec as P

F = 26
BLOCK = 128
VECS = F + 1
LANES = 128
CHAINS = 4
UNROLL = 32
VMEM = 32 << 20
SMEM_SPEC = pl.BlockSpec(memory_space=pltpu.SMEM)
ANY_SPEC = pl.BlockSpec(memory_space=pl.ANY)
HBM_SPEC = pl.BlockSpec(memory_space=pltpu.HBM)
VMEM_SPEC = pl.BlockSpec(memory_space=pltpu.VMEM)


def fill_kernel(slot_ref, block_ref, cache_ref, fills_ref, out_ref, sem):
    def of_block(ref, index):
        return ref.at[pl.ds(pl.multiple_of(index * BLOCK, BLOCK), BLOCK)]

    n_slots = out_ref.shape[0] // BLOCK
    n_fills = slot_ref.shape[0]

    def kept(index):
        hit = slot_ref[0] == index
        for k in range(1, n_fills):
            hit = jnp.logical_or(hit, slot_ref[k] == index)
        return jnp.logical_not(hit)

    def cache_copy(index):
        return pltpu.make_async_copy(of_block(cache_ref, index), of_block(out_ref, index), sem.at[index])

    def fill_copy(k):
        slot = jnp.minimum(slot_ref[k], n_slots - 1)
        return pltpu.make_async_copy(
            of_block(fills_ref, block_ref[k]), of_block(out_ref, slot), sem.at[n_slots + k]
        )

    for k in range(n_fills):
        pl.when(slot_ref[k] < n_slots)(lambda k=k: fill_copy(k).start())
    for index in range(n_slots):
        pl.when(kept(index))(lambda index=index: cache_copy(index).start())
    for index in range(n_slots):
        pl.when(kept(index))(lambda index=index: cache_copy(index).wait())
    for k in range(n_fills):
        pl.when(slot_ref[k] < n_slots)(lambda k=k: fill_copy(k).wait())


def fill(cache_rows, fills, miss_slot, fill_block):
    n_sems = cache_rows.shape[0] // BLOCK + miss_slot.shape[0]
    return pl.pallas_call(
        fill_kernel,
        out_shape=jax.ShapeDtypeStruct(cache_rows.shape, cache_rows.dtype),
        in_specs=[SMEM_SPEC] * 2 + [ANY_SPEC] * 2,
        out_specs=VMEM_SPEC,
        scratch_shapes=[pltpu.SemaphoreType.DMA((n_sems,))],
        name="fill",
    )(miss_slot, fill_block, cache_rows, fills)


def gate_kernel(*refs):
    pass


def gate(arrays, after):
    n_arrays = len(arrays)
    return pl.pallas_call(
        gate_kernel,
        out_shape=[jax.ShapeDtypeStruct(one.shape, one.dtype) for one in arrays],
        in_specs=[ANY_SPEC] * n_arrays + [SMEM_SPEC],
        out_specs=[ANY_SPEC] * n_arrays,
        input_output_aliases={index: index for index in range(n_arrays)},
        compiler_params=pltpu.CompilerParams(vmem_limit_bytes=1 << 20),
        name="gate",
    )(*arrays, after)


def pool_shards(first, rows, entry_refs, entry_held, count_ref, shards, sems, held, table, sums):
    cap = entry_held[0].shape[0] // 8
    copies = [
        pltpu.make_async_copy(ref.at[pl.ds(first * cap, 8 * cap)], to, sems.at[len(shards) + index])
        for index, (ref, to) in enumerate(zip(entry_refs, entry_held))
    ]
    copies += [pltpu.make_async_copy(ref, held.at[s], sems.at[s]) for s, ref in enumerate(shards)]
    for copy in copies:
        copy.start()
    yield
    for copy in copies[:2]:
        copy.wait()
    slot_ref, bag_ref = entry_held
    for s, copy in enumerate(copies[2:]):
        copy.wait()
        table[...] = held[s].astype(jnp.float32)
        row = rows[s]

        def add_entries(step, _):
            start = row * cap + step * UNROLL
            for group in range(UNROLL // CHAINS):
                entries = [start + group * CHAINS + k for k in range(CHAINS)]
                slots = [slot_ref[e] for e in entries]
                bags = [bag_ref[e] for e in entries]
                found = [table[pl.ds(slot, 1), :] for slot in slots]
                olds = [sums[k][pl.ds(bags[k], 1), :] for k in range(CHAINS)]
                for k in range(CHAINS):
                    sums[k][pl.ds(bags[k], 1), :] = olds[k] + found[k]
            return 0

        lax.fori_loop(0, count_ref[first + row], add_entries, 0)


def pool_kernel(first, rows, is_first, count_ref, slot_ref, bag_ref, *refs):
    shards, refs = refs[: len(rows)], refs[len(rows) :]
    if not is_first:
        refs = refs[CHAINS:]
    sums, (done, *entry_held, held, table, sems) = refs[:CHAINS], refs[CHAINS:]
    pooling = pool_shards(
        first, rows, (slot_ref, bag_ref), entry_held, count_ref, shards, sems, held, table, sums
    )
    next(pooling)
    if is_first:
        for one in sums:
            one[...] = jnp.zeros_like(one)
    for _ in pooling:
        pass
    done[0] = 0


def interact(sums, dense_ref, masked, queries):
    lane = lax.broadcasted_iota(jnp.int32, (8, 256), 1)
    row = lax.broadcasted_iota(jnp.int32, (8, 256), 0)
    own_query = (lane & 7) == row

    def sixteen_queries(step, _):
        dense = dense_ref[pl.ds(pl.multiple_of(step * 16, 16), 16), :].astype(jnp.float32)
        halves = []
        for half in range(2):
            query = pl.multiple_of(step * 16 + half * 8, 8)
            vectors = [dense[half * 8 : half * 8 + 8]]
            for feature in range(F):
                rows = pl.ds(pl.multiple_of(feature * queries + query, 8), 8)
                total = sums[0][rows, :]
                for one in sums[1:]:
                    total = total + one[rows, :]
                vectors.append(total)
            vectors += [jnp.zeros((8, LANES), jnp.float32)] * (32 - VECS)
            stacked = jnp.concatenate(vectors, axis=0).astype(jnp.bfloat16)
            halves.append(
                lax.dot_general(
                    stacked, stacked, (((1,), (1,)), ((), ())), preferred_element_type=jnp.float32
                )
            )
        for i in range(F):
            pair = [
                jnp.where(own_query, products[8 * i : 8 * i + 8, :], 0.0) for products in halves
            ]
            masked[i, pl.ds(pl.multiple_of(step * 16, 16), 16), :] = jnp.concatenate(
                pair, axis=0
            ).astype(jnp.bfloat16)
        return 0

    lax.fori_loop(0, queries // 16, sixteen_queries, 0)


def inter_columns(masked, dense_ref, inter, queries):
    spread = lax.broadcasted_iota(jnp.int32, (256, LANES), 0) // 8
    vector = lax.broadcasted_iota(jnp.int32, (256, LANES), 1)
    pick = jnp.where(spread == vector, 1.0, 0.0).astype(jnp.bfloat16)
    lane = lax.broadcasted_iota(jnp.int32, (queries, LANES), 1)
    tiles = [jnp.zeros((queries, LANES), jnp.float32) for _ in range(3)]
    first = 0
    for i in range(F):
        length = F - i
        picked = jnp.dot(masked[i], pick, preferred_element_type=jnp.float32)
        shift = (first - (i + 1)) % LANES
        if shift:
            picked = pltpu.roll(picked, shift, 1)
        for tile in range(3):
            low, high = max(first, tile * LANES), min(first + length, (tile + 1) * LANES)
            if low < high:
                inside = jnp.logical_and(lane >= low - tile * LANES, lane < high - tile * LANES)
                tiles[tile] = jnp.where(inside, picked, tiles[tile])
        first += length
    inter[:, :LANES] = dense_ref[...]
    for tile in range(3):
        inter[:, (tile + 1) * LANES : (tile + 2) * LANES] = tiles[tile].astype(jnp.bfloat16)


def final_kernel(first, n_shards, with_head, count_ref, slot_ref, bag_ref, *refs):
    shards, refs = refs[:n_shards], refs[n_shards:]
    old_sums, dense_ref, refs = refs[:CHAINS], refs[CHAINS], refs[CHAINS + 1 :]
    if with_head:
        w_first, w_second, w_out, logits, *refs = refs
    else:
        inter, *refs = refs
    refs = refs[CHAINS:]
    if with_head:
        inter, first_held, second_held, weight_sems, *refs = refs
        weights = [
            pltpu.make_async_copy(w_first, first_held, weight_sems.at[0]),
            pltpu.make_async_copy(w_second, second_held, weight_sems.at[1]),
        ]
        for copy in weights:
            copy.start()
    masked, *entry_held, held, table, sems = refs
    queries = dense_ref.shape[0]
    for _ in pool_shards(
        first, (0, 1), (slot_ref, bag_ref), entry_held, count_ref, shards, sems, held, table, old_sums
    ):
        pass
    interact(old_sums, dense_ref, masked, queries)
    inter_columns(masked, dense_ref, inter, queries)
    if not with_head:
        return
    for copy in weights:
        copy.wait()
    step = LANES
    inputs = first_held.shape[0]
    for part in range(queries // step):
        rows = slice(part * step, (part + 1) * step)
        hidden = jnp.dot(inter[rows, :inputs], first_held[...], preferred_element_type=jnp.float32)
        hidden = jnp.maximum(hidden, 0.0).astype(jnp.bfloat16)
        second = jnp.dot(hidden, second_held[...], preferred_element_type=jnp.float32)
        scored = jnp.maximum(second, 0.0) * w_out[...]
        folded = scored[:, :LANES]
        for tile in range(1, scored.shape[1] // LANES):
            folded = folded + scored[:, tile * LANES : (tile + 1) * LANES]
        logits[rows] = jnp.sum(folded.T, axis=0)


def pool_scratch(n_shards, shard_rows, cap):
    return [
        pltpu.SMEM((8 * cap,), jnp.int32),
        pltpu.SMEM((8 * cap,), jnp.int32),
        pltpu.VMEM((n_shards, shard_rows, LANES), jnp.bfloat16),
        pltpu.VMEM((shard_rows, LANES), jnp.float32),
        pltpu.SemaphoreType.DMA((n_shards + 2,)),
    ]


def pool(first, entries, shards, sums, sum_rows, rows=(0, 1)):
    n_shards = len(shards)
    is_first = sums is None
    sums = [] if is_first else sums
    *sums, done = pl.pallas_call(
        functools.partial(pool_kernel, first, rows, is_first),
        out_shape=[pltpu.VMEM((sum_rows, LANES), jnp.float32)] * CHAINS
        + [jax.ShapeDtypeStruct((1,), jnp.int32)],
        in_specs=[SMEM_SPEC] + [HBM_SPEC] * 2 + [ANY_SPEC] * n_shards + [VMEM_SPEC] * len(sums),
        out_specs=[VMEM_SPEC] * CHAINS + [SMEM_SPEC],
        input_output_aliases={3 + n_shards + k: k for k in range(len(sums))},
        scratch_shapes=pool_scratch(n_shards, shards[0].shape[0], entries[1].shape[0] // entries[0].shape[0]),
        compiler_params=pltpu.CompilerParams(vmem_limit_bytes=VMEM),
        cost_estimate=pl.CostEstimate(flops=0, bytes_accessed=n_shards * 6_000_000, transcendentals=0),
        name="pool",
    )(*entries, *shards, *sums)
    return sums, done


def finish(first, entries, shards, sums, dense_rows, head):
    n_shards = len(shards)
    queries = dense_rows.shape[0]
    width = 4 * LANES
    masked = pltpu.VMEM((F, queries, 256), jnp.bfloat16)
    if head is None:
        head_args, head_specs = [], []
        out_shape = jax.ShapeDtypeStruct((queries, width), jnp.bfloat16)
        scratch = [masked]
    else:
        head_args, head_specs = list(head), [HBM_SPEC, HBM_SPEC, VMEM_SPEC]
        out_shape = jax.ShapeDtypeStruct((queries,), jnp.float32)
        scratch = [
            pltpu.VMEM((queries, width), jnp.bfloat16),
            pltpu.VMEM(head[0].shape, jnp.bfloat16),
            pltpu.VMEM(head[1].shape, jnp.bfloat16),
            pltpu.SemaphoreType.DMA((2,)),
            masked,
        ]
    out = pl.pallas_call(
        functools.partial(final_kernel, first, n_shards, head is not None),
        out_shape=[out_shape] + [pltpu.VMEM(one.shape, one.dtype) for one in sums],
        in_specs=[SMEM_SPEC] + [HBM_SPEC] * 2 + [ANY_SPEC] * n_shards + [VMEM_SPEC] * (CHAINS + 1) + head_specs,
        out_specs=[VMEM_SPEC] * (CHAINS + 1),
        input_output_aliases={3 + n_shards + k: 1 + k for k in range(CHAINS)},
        scratch_shapes=scratch + pool_scratch(n_shards, shards[0].shape[0], entries[1].shape[0] // entries[0].shape[0]),
        compiler_params=pltpu.CompilerParams(vmem_limit_bytes=VMEM),
        name="finish",
    )(*entries, *shards, *sums, dense_rows, *head_args)
    return out[0]


def per_device(
    n_planes,
    cache_rows,
    store_rows,
    miss_block,
    miss_slot,
    lookup_slot,
    lookup_bag,
    dense_rows,
    w_first,
    w_second,
    w_out,
):
    emb_width = cache_rows.shape[1]
    queries = dense_rows.shape[0]
    bags = queries * F
    owners = lax.axis_size("owner")
    n_shards = n_planes * 8

    if owners == 1:
        fills, fill_block = store_rows, miss_block[0]
    else:
        fills = store_rows.reshape(-1, BLOCK, emb_width)[miss_block[0]]
        fills = lax.all_gather(fills, "owner", axis=0, tiled=True)
        fill_block = jnp.arange(fills.shape[0], dtype=jnp.int32)
        fills = fills.reshape(-1, emb_width)
    own = fill(cache_rows, fills, miss_slot[0], fill_block)

    def device(z, y, x, core):
        return ((z * 2 + y) * 2 + x) * 2 + core

    def hop(move):
        pairs = []
        for index in range(n_shards):
            at = (index // 8, index // 4 % 2, index // 2 % 2, index % 2)
            pairs.append((index, device(*move(*at))))
        return lambda array: lax.ppermute(array, "cache", pairs)

    next_plane = hop(lambda z, y, x, core: ((z + 1) % n_planes, y, x, core))
    first_hop = hop(lambda z, y, x, core: (z, y, 1 - x, core) if core == 0 else (z, 1 - y, x, core))
    second_hop = hop(lambda z, y, x, core: (z, 1 - y, x, core) if core == 0 else (z, y, 1 - x, core))
    other_core = hop(lambda z, y, x, core: (z, y, x, 1 - core))

    me = lax.axis_index("cache")
    z, y, x, core = me // 8, me // 4 % 2, me // 2 % 2, me % 2

    def origin(shift, flip_first, flip_second, side):
        flip_x = jnp.where(side == 0, flip_first, flip_second)
        flip_y = jnp.where(side == 0, flip_second, flip_first)
        return device((z - shift) % n_planes, y ^ flip_y, x ^ flip_x, side)

    def both_cores(shift, *flips):
        return [origin(shift, *flips, side) for side in (core, 1 - core)]

    unused = [0] * 6
    order = both_cores(0, 0, 0) + unused
    for shift in range(n_planes):
        before, after = max(shift - 1, 0), min(shift + 1, n_planes - 1)
        order += both_cores(shift, 1, 0) + both_cores(shift, 0, 1)
        order += both_cores(before, 1, 1) + both_cores(after, 0, 0)
    order += both_cores(n_planes - 1, 1, 1) + unused
    order = jnp.stack(order)
    cap = lookup_slot.shape[2]
    cap += -cap % LANES
    spare = ((0, 0), (0, cap - lookup_slot.shape[2]))
    slots = jnp.pad(lookup_slot[0], spare)[order]
    bag_ids = jnp.pad(lookup_bag[0], spare, constant_values=bags)[order]
    used = jnp.sum((bag_ids < bags).astype(jnp.int32), axis=1)
    steps = (used + UNROLL - 1) // UNROLL
    sum_rows = bags + 8
    places = jnp.where(bag_ids < bags, bag_ids % F * queries + bag_ids // F, bags)
    entries = (steps, slots.reshape(-1), places.reshape(-1))

    def of_chip(array):
        return [array, other_core(array)]

    crossed, turned, next_piece = first_hop(own), second_hop(own), next_plane(own)
    sums, _ = pool(0, entries, of_chip(own), None, sum_rows)
    far = []
    for shift in range(n_planes):
        last = shift == n_planes - 1
        near = of_chip(crossed) + of_chip(turned)
        next_far = second_hop(crossed)
        passed = [next_far]
        if not last:
            passed += [first_hop(next_piece), second_hop(next_piece)]
            piece = of_chip(next_piece)
            if shift < n_planes - 2:
                passed.append(next_plane(next_piece))
        else:
            piece = []
        if shift == 0:
            shards, rows = near + piece, [0, 1, 2, 3, 6, 7]
        else:
            shards, rows = near + far + piece, list(range(6 + len(piece)))
        sums, done = pool(8 * shift + 8, entries, shards, sums, sum_rows, rows)
        next_far, *passed = gate(passed, done)
        far = of_chip(next_far)
        if not last:
            crossed, turned, *next_piece = passed
            next_piece = next_piece[0] if next_piece else None
    args = (8 * n_planes + 8, entries, far, sums, dense_rows)
    if owners == 1:
        return finish(*args, (w_first, w_second, w_out.reshape(1, -1)))
    inter_in = finish(*args, None)[:, : w_first.shape[0]]
    group_inputs = lax.all_gather(inter_in, "owner", axis=0, tiled=True)
    hidden = jax.nn.relu(jnp.dot(group_inputs, w_first, preferred_element_type=jnp.float32))
    second = lax.psum_scatter(
        jnp.dot(hidden.astype(jnp.bfloat16), w_second, preferred_element_type=jnp.float32),
        "owner",
        scatter_dimension=0,
        tiled=True,
    )
    return jnp.sum(jax.nn.relu(second) * w_out, axis=1)


def solution(mesh):
    in_specs = (
        P(("rep", "cache"), None),
        P(("rep", "cache", "owner"), None),
        P(("rep", "cache", "owner"), None),
        P(("rep", "cache"), None),
        P(("rep", "cache", "owner"), None, None),
        P(("rep", "cache", "owner"), None, None),
        P(("rep", "cache", "owner"), None),
        P(None, "owner"),
        P("owner", None),
        P(),
    )
    out_specs = P(("rep", "cache", "owner"))
    return jax.shard_map(
        functools.partial(per_device, mesh.shape["cache"] // 8),
        mesh=mesh,
        in_specs=in_specs,
        out_specs=out_specs,
        check_vma=False,
    )
```

```python
import functools

import jax
import jax.numpy as jnp
from jax import lax
from jax.experimental import pallas as pl
from jax.experimental.pallas import tpu as pltpu
from jax.sharding import PartitionSpec as P

F = 26
BLOCK = 128
VECS = F + 1
LANES = 128
CHAINS = 4
UNROLL = 32
VMEM = 18 << 20
SMEM_SPEC = pl.BlockSpec(memory_space=pltpu.SMEM)
ANY_SPEC = pl.BlockSpec(memory_space=pl.ANY)
HBM_SPEC = pl.BlockSpec(memory_space=pltpu.HBM)
VMEM_SPEC = pl.BlockSpec(memory_space=pltpu.VMEM)


def fill_kernel(slot_ref, block_ref, cache_ref, fills_ref, out_ref, sem):
    def of_block(ref, index):
        return ref.at[pl.ds(pl.multiple_of(index * BLOCK, BLOCK), BLOCK)]

    n_slots = out_ref.shape[0] // BLOCK
    n_fills = slot_ref.shape[0]

    def kept(index):
        hit = slot_ref[0] == index
        for k in range(1, n_fills):
            hit = jnp.logical_or(hit, slot_ref[k] == index)
        return jnp.logical_not(hit)

    def cache_copy(index):
        return pltpu.make_async_copy(of_block(cache_ref, index), of_block(out_ref, index), sem.at[index])

    def fill_copy(k):
        slot = jnp.minimum(slot_ref[k], n_slots - 1)
        return pltpu.make_async_copy(
            of_block(fills_ref, block_ref[k]), of_block(out_ref, slot), sem.at[n_slots + k]
        )

    for k in range(n_fills):
        pl.when(slot_ref[k] < n_slots)(lambda k=k: fill_copy(k).start())
    for index in range(n_slots):
        pl.when(kept(index))(lambda index=index: cache_copy(index).start())
    for index in range(n_slots):
        pl.when(kept(index))(lambda index=index: cache_copy(index).wait())
    for k in range(n_fills):
        pl.when(slot_ref[k] < n_slots)(lambda k=k: fill_copy(k).wait())


def fill(cache_rows, fills, miss_slot, fill_block):
    n_sems = cache_rows.shape[0] // BLOCK + miss_slot.shape[0]
    return pl.pallas_call(
        fill_kernel,
        out_shape=jax.ShapeDtypeStruct(cache_rows.shape, cache_rows.dtype),
        in_specs=[SMEM_SPEC] * 2 + [ANY_SPEC] * 2,
        out_specs=VMEM_SPEC,
        scratch_shapes=[pltpu.SemaphoreType.DMA((n_sems,))],
        name="fill",
    )(miss_slot, fill_block, cache_rows, fills)


PICK = [1]


def gate_kernel(*refs):
    pass


def gate(arrays, after):
    n_arrays = len(arrays)
    if not arrays:
        return []
    return pl.pallas_call(
        gate_kernel,
        out_shape=[jax.ShapeDtypeStruct(one.shape, one.dtype) for one in arrays],
        in_specs=[ANY_SPEC] * n_arrays + [SMEM_SPEC],
        out_specs=[ANY_SPEC] * n_arrays,
        input_output_aliases={index: index for index in range(n_arrays)},
        compiler_params=pltpu.CompilerParams(vmem_limit_bytes=1 << 20),
        name="gate",
    )(*arrays, after)


def pool_shards(first, rows, entry_refs, entry_held, count_ref, shards, sems, held, table, sums):
    cap = entry_held[0].shape[0] // 8
    copies = [
        pltpu.make_async_copy(ref.at[pl.ds(first * cap, 8 * cap)], to, sems.at[len(shards) + index])
        for index, (ref, to) in enumerate(zip(entry_refs, entry_held))
    ]
    copies += [pltpu.make_async_copy(ref, held.at[s], sems.at[s]) for s, ref in enumerate(shards)]
    for copy in copies:
        copy.start()
    yield
    for copy in copies[:2]:
        copy.wait()
    slot_ref, bag_ref = entry_held
    for s, copy in enumerate(copies[2:]):
        copy.wait()
        table[...] = held[s].astype(jnp.float32)
        row = rows[s]

        def add_entries(step, _):
            start = row * cap + step * UNROLL
            for group in range(UNROLL // CHAINS):
                entries = [start + group * CHAINS + k for k in range(CHAINS)]
                slots = [slot_ref[e] for e in entries]
                bags = [bag_ref[e] for e in entries]
                found = [table[pl.ds(slot, 1), :] for slot in slots]
                olds = [sums[k][pl.ds(bags[k], 1), :] for k in range(CHAINS)]
                for k in range(CHAINS):
                    sums[k][pl.ds(bags[k], 1), :] = olds[k] + found[k]
            return 0

        lax.fori_loop(0, count_ref[first + row], add_entries, 0)


def pool_kernel(first, rows, is_first, count_ref, slot_ref, bag_ref, *refs):
    shards, refs = refs[: len(rows)], refs[len(rows) :]
    if not is_first:
        refs = refs[CHAINS:]
    sums, (done, *entry_held, held, table, sems) = refs[:CHAINS], refs[CHAINS:]
    pooling = pool_shards(
        first, rows, (slot_ref, bag_ref), entry_held, count_ref, shards, sems, held, table, sums
    )
    next(pooling)
    if is_first:
        for one in sums:
            one[...] = jnp.zeros_like(one)
    for _ in pooling:
        pass
    done[0] = 0


def interact(sums, dense_ref, masked, queries):
    lane = lax.broadcasted_iota(jnp.int32, (8, 256), 1)
    row = lax.broadcasted_iota(jnp.int32, (8, 256), 0)
    own_query = (lane & 7) == row

    def sixteen_queries(step, _):
        dense = dense_ref[pl.ds(pl.multiple_of(step * 16, 16), 16), :].astype(jnp.float32)
        halves = []
        for half in range(2):
            query = pl.multiple_of(step * 16 + half * 8, 8)
            vectors = [dense[half * 8 : half * 8 + 8]]
            for feature in range(F):
                rows = pl.ds(pl.multiple_of(feature * queries + query, 8), 8)
                total = sums[0][rows, :]
                for one in sums[1:]:
                    total = total + one[rows, :]
                vectors.append(total)
            vectors += [jnp.zeros((8, LANES), jnp.float32)] * (32 - VECS)
            stacked = jnp.concatenate(vectors, axis=0).astype(jnp.bfloat16)
            halves.append(
                lax.dot_general(
                    stacked, stacked, (((1,), (1,)), ((), ())), preferred_element_type=jnp.float32
                )
            )
        for i in range(F):
            pair = [
                jnp.where(own_query, products[8 * i : 8 * i + 8, :], 0.0) for products in halves
            ]
            masked[i, pl.ds(pl.multiple_of(step * 16, 16), 16), :] = jnp.concatenate(
                pair, axis=0
            ).astype(jnp.bfloat16)
        return 0

    lax.fori_loop(0, queries // 16, sixteen_queries, 0, unroll=4)


def inter_columns(masked, dense_ref, inter, queries):
    spread = lax.broadcasted_iota(jnp.int32, (256, LANES), 0) // 8
    vector = lax.broadcasted_iota(jnp.int32, (256, LANES), 1)
    pick = jnp.where(spread == vector, 1.0, 0.0).astype(jnp.bfloat16)
    lane = lax.broadcasted_iota(jnp.int32, (queries, LANES), 1)
    tiles = [jnp.zeros((queries, LANES), jnp.float32) for _ in range(3)]
    first = 0
    for i in range(F):
        length = F - i
        picked = jnp.dot(masked[i], pick, preferred_element_type=jnp.float32)
        shift = (first - (i + 1)) % LANES
        if shift:
            picked = pltpu.roll(picked, shift, 1)
        for tile in range(3):
            low, high = max(first, tile * LANES), min(first + length, (tile + 1) * LANES)
            if low < high:
                inside = jnp.logical_and(lane >= low - tile * LANES, lane < high - tile * LANES)
                tiles[tile] = jnp.where(inside, picked, tiles[tile])
        first += length
    inter[:, :LANES] = dense_ref[...]
    for tile in range(3):
        inter[:, (tile + 1) * LANES : (tile + 2) * LANES] = tiles[tile].astype(jnp.bfloat16)


def final_kernel(first, n_shards, with_head, count_ref, slot_ref, bag_ref, *refs):
    shards, refs = refs[:n_shards], refs[n_shards:]
    old_sums, dense_ref, refs = refs[:CHAINS], refs[CHAINS], refs[CHAINS + 1 :]
    if with_head:
        w_first, w_second, w_out, logits, *refs = refs
    else:
        inter, *refs = refs
    refs = refs[CHAINS:]
    if with_head:
        inter, first_held, second_held, weight_sems, *refs = refs
        weights = [
            pltpu.make_async_copy(w_first, first_held, weight_sems.at[0]),
            pltpu.make_async_copy(w_second, second_held, weight_sems.at[1]),
        ]
        for copy in weights:
            copy.start()
    masked, *entry_held, held, table, sems = refs
    queries = dense_ref.shape[0]
    for _ in pool_shards(
        first, (0, 1), (slot_ref, bag_ref), entry_held, count_ref, shards, sems, held, table, old_sums
    ):
        pass
    interact(old_sums, dense_ref, masked, queries)
    inter_columns(masked, dense_ref, inter, queries)
    if not with_head:
        return
    for copy in weights:
        copy.wait()
    step = LANES
    inputs = first_held.shape[0]
    for part in range(queries // step):
        rows = slice(part * step, (part + 1) * step)
        hidden = jnp.dot(inter[rows, :inputs], first_held[...], preferred_element_type=jnp.float32)
        hidden = jnp.maximum(hidden, 0.0).astype(jnp.bfloat16)
        second = jnp.dot(hidden, second_held[...], preferred_element_type=jnp.float32)
        scored = jnp.maximum(second, 0.0) * w_out[...]
        folded = scored[:, :LANES]
        for tile in range(1, scored.shape[1] // LANES):
            folded = folded + scored[:, tile * LANES : (tile + 1) * LANES]
        logits[rows] = jnp.sum(folded.T, axis=0)


def pool_scratch(n_shards, shard_rows, cap):
    return [
        pltpu.SMEM((8 * cap,), jnp.int32),
        pltpu.SMEM((8 * cap,), jnp.int32),
        pltpu.VMEM((n_shards, shard_rows, LANES), jnp.bfloat16),
        pltpu.VMEM((shard_rows, LANES), jnp.float32),
        pltpu.SemaphoreType.DMA((n_shards + 2,)),
    ]


def pool(first, entries, shards, sums, sum_rows, rows=(0, 1)):
    n_shards = len(shards)
    is_first = sums is None
    sums = [] if is_first else sums
    *sums, done = pl.pallas_call(
        functools.partial(pool_kernel, first, rows, is_first),
        out_shape=[pltpu.VMEM((sum_rows, LANES), jnp.float32)] * CHAINS
        + [jax.ShapeDtypeStruct((1,), jnp.int32)],
        in_specs=[SMEM_SPEC] + [HBM_SPEC] * 2 + [ANY_SPEC] * n_shards + [VMEM_SPEC] * len(sums),
        out_specs=[VMEM_SPEC] * CHAINS + [SMEM_SPEC],
        input_output_aliases={3 + n_shards + k: k for k in range(len(sums))},
        scratch_shapes=pool_scratch(n_shards, shards[0].shape[0], entries[1].shape[0] // entries[0].shape[0]),
        compiler_params=pltpu.CompilerParams(vmem_limit_bytes=VMEM),
        cost_estimate=pl.CostEstimate(flops=0, bytes_accessed=n_shards * 3000000, transcendentals=0),
        name="pool",
    )(*entries, *shards, *sums)
    return sums, done


def finish(first, entries, shards, sums, dense_rows, head):
    n_shards = len(shards)
    queries = dense_rows.shape[0]
    width = 4 * LANES
    masked = pltpu.VMEM((F, queries, 256), jnp.bfloat16)
    if head is None:
        head_args, head_specs = [], []
        out_shape = jax.ShapeDtypeStruct((queries, width), jnp.bfloat16)
        scratch = [masked]
    else:
        head_args, head_specs = list(head), [HBM_SPEC, HBM_SPEC, VMEM_SPEC]
        out_shape = jax.ShapeDtypeStruct((queries,), jnp.float32)
        scratch = [
            pltpu.VMEM((queries, width), jnp.bfloat16),
            pltpu.VMEM(head[0].shape, jnp.bfloat16),
            pltpu.VMEM(head[1].shape, jnp.bfloat16),
            pltpu.SemaphoreType.DMA((2,)),
            masked,
        ]
    out = pl.pallas_call(
        functools.partial(final_kernel, first, n_shards, head is not None),
        out_shape=[out_shape] + [pltpu.VMEM(one.shape, one.dtype) for one in sums],
        in_specs=[SMEM_SPEC] + [HBM_SPEC] * 2 + [ANY_SPEC] * n_shards + [VMEM_SPEC] * (CHAINS + 1) + head_specs,
        out_specs=[VMEM_SPEC] * (CHAINS + 1),
        input_output_aliases={3 + n_shards + k: 1 + k for k in range(CHAINS)},
        scratch_shapes=scratch + pool_scratch(n_shards, shards[0].shape[0], entries[1].shape[0] // entries[0].shape[0]),
        compiler_params=pltpu.CompilerParams(vmem_limit_bytes=VMEM),
        name="finish",
    )(*entries, *shards, *sums, dense_rows, *head_args)
    return out[0]


def per_device(
    n_planes,
    cache_rows,
    store_rows,
    miss_block,
    miss_slot,
    lookup_slot,
    lookup_bag,
    dense_rows,
    w_first,
    w_second,
    w_out,
):
    emb_width = cache_rows.shape[1]
    queries = dense_rows.shape[0]
    bags = queries * F
    owners = lax.axis_size("owner")
    n_shards = n_planes * 8

    if owners == 1:
        fills, fill_block = store_rows, miss_block[0]
    else:
        fills = store_rows.reshape(-1, BLOCK, emb_width)[miss_block[0]]
        fills = lax.all_gather(fills, "owner", axis=0, tiled=True)
        fill_block = jnp.arange(fills.shape[0], dtype=jnp.int32)
        fills = fills.reshape(-1, emb_width)
    own = fill(cache_rows, fills, miss_slot[0], fill_block)

    def device(z, y, x, core):
        return ((z * 2 + y) * 2 + x) * 2 + core

    def hop(move):
        pairs = []
        for index in range(n_shards):
            at = (index // 8, index // 4 % 2, index // 2 % 2, index % 2)
            pairs.append((index, device(*move(*at))))
        return lambda array: lax.ppermute(array, "cache", pairs)

    next_plane = hop(lambda z, y, x, core: ((z + 1) % n_planes, y, x, core))
    first_hop = hop(lambda z, y, x, core: (z, y, 1 - x, core) if core == 0 else (z, 1 - y, x, core))
    second_hop = hop(lambda z, y, x, core: (z, 1 - y, x, core) if core == 0 else (z, y, 1 - x, core))
    other_core = hop(lambda z, y, x, core: (z, y, x, 1 - core))

    me = lax.axis_index("cache")
    z, y, x, core = me // 8, me // 4 % 2, me // 2 % 2, me % 2

    def origin(shift, flip_first, flip_second, side):
        flip_x = jnp.where(side == 0, flip_first, flip_second)
        flip_y = jnp.where(side == 0, flip_second, flip_first)
        return device((z - shift) % n_planes, y ^ flip_y, x ^ flip_x, side)

    def both_cores(shift, *flips):
        return [origin(shift, *flips, side) for side in (core, 1 - core)]

    unused = [0] * 6
    order = both_cores(0, 0, 0) + unused
    for shift in range(n_planes):
        before, after = max(shift - 1, 0), min(shift + 1, n_planes - 1)
        order += both_cores(shift, 1, 0) + both_cores(shift, 0, 1)
        order += both_cores(before, 1, 1) + both_cores(after, 0, 0)
    order += both_cores(n_planes - 1, 1, 1) + unused
    order = jnp.stack(order)
    cap = lookup_slot.shape[2]
    cap += -cap % LANES
    spare = ((0, 0), (0, cap - lookup_slot.shape[2]))
    slots = jnp.pad(lookup_slot[0], spare)[order]
    bag_ids = jnp.pad(lookup_bag[0], spare, constant_values=bags)[order]
    used = jnp.sum((bag_ids < bags).astype(jnp.int32), axis=1)
    steps = (used + UNROLL - 1) // UNROLL
    sum_rows = bags + 8
    places = jnp.where(bag_ids < bags, bag_ids % F * queries + bag_ids // F, bags)
    entries = (steps, slots.reshape(-1), places.reshape(-1))

    def of_chip(array):
        return [array, other_core(array)]

    crossed, turned, next_piece = first_hop(own), second_hop(own), next_plane(own)
    sums, done = pool(0, entries, of_chip(own), None, sum_rows)
    (next_piece,) = gate([next_piece], done)
    far = []
    for shift in range(n_planes):
        last = shift == n_planes - 1
        near = of_chip(crossed) + of_chip(turned)
        next_far = next_plane(far[0]) if shift == n_planes - 2 else second_hop(crossed)
        passed = [next_far]
        if not last:
            passed += [first_hop(next_piece), second_hop(next_piece)]
            piece = of_chip(next_piece)
            if shift < n_planes - 2:
                passed.append(next_plane(next_piece))
        else:
            piece = []
        if shift == 0:
            shards, rows = near + piece, [0, 1, 2, 3, 6, 7]
        else:
            shards, rows = near + far + piece, list(range(6 + len(piece)))
        sums, done = pool(8 * shift + 8, entries, shards, sums, sum_rows, rows)
        chosen = [0] if last else [index for index in PICK if index < len(passed)]
        for index, one in zip(chosen, gate([passed[index] for index in chosen], done)):
            passed[index] = one
        next_far, *passed = passed
        far = of_chip(next_far)
        if not last:
            crossed, turned, *next_piece = passed
            next_piece = next_piece[0] if next_piece else None
    args = (8 * n_planes + 8, entries, far, sums, dense_rows)
    if owners == 1:
        return finish(*args, (w_first, w_second, w_out.reshape(1, -1)))
    inter_in = finish(*args, None)[:, : w_first.shape[0]]
    group_inputs = lax.all_gather(inter_in, "owner", axis=0, tiled=True)
    hidden = jax.nn.relu(jnp.dot(group_inputs, w_first, preferred_element_type=jnp.float32))
    second = lax.psum_scatter(
        jnp.dot(hidden.astype(jnp.bfloat16), w_second, preferred_element_type=jnp.float32),
        "owner",
        scatter_dimension=0,
        tiled=True,
    )
    return jnp.sum(jax.nn.relu(second) * w_out, axis=1)


def solution(mesh):
    in_specs = (
        P(("rep", "cache"), None),
        P(("rep", "cache", "owner"), None),
        P(("rep", "cache", "owner"), None),
        P(("rep", "cache"), None),
        P(("rep", "cache", "owner"), None, None),
        P(("rep", "cache", "owner"), None, None),
        P(("rep", "cache", "owner"), None),
        P(None, "owner"),
        P("owner", None),
        P(),
    )
    out_specs = P(("rep", "cache", "owner"))
    return jax.shard_map(
        functools.partial(per_device, mesh.shape["cache"] // 8),
        mesh=mesh,
        in_specs=in_specs,
        out_specs=out_specs,
        check_vma=False,
    )
```

```python
import functools

import jax
import jax.numpy as jnp
from jax import lax
from jax.experimental import pallas as pl
from jax.experimental.pallas import tpu as pltpu
from jax.sharding import PartitionSpec as P

F = 26
BLOCK = 128
VECS = F + 1
LANES = 128
CHAINS = 4
UNROLL = 32
VMEM = 18 << 20
SMEM_SPEC = pl.BlockSpec(memory_space=pltpu.SMEM)
ANY_SPEC = pl.BlockSpec(memory_space=pl.ANY)
HBM_SPEC = pl.BlockSpec(memory_space=pltpu.HBM)
VMEM_SPEC = pl.BlockSpec(memory_space=pltpu.VMEM)


def fill_kernel(slot_ref, block_ref, cache_ref, fills_ref, out_ref, sem):
    def of_block(ref, index):
        return ref.at[pl.ds(pl.multiple_of(index * BLOCK, BLOCK), BLOCK)]

    n_slots = out_ref.shape[0] // BLOCK
    n_fills = slot_ref.shape[0]

    def kept(index):
        hit = slot_ref[0] == index
        for k in range(1, n_fills):
            hit = jnp.logical_or(hit, slot_ref[k] == index)
        return jnp.logical_not(hit)

    def cache_copy(index):
        return pltpu.make_async_copy(of_block(cache_ref, index), of_block(out_ref, index), sem.at[index])

    def fill_copy(k):
        slot = jnp.minimum(slot_ref[k], n_slots - 1)
        return pltpu.make_async_copy(
            of_block(fills_ref, block_ref[k]), of_block(out_ref, slot), sem.at[n_slots + k]
        )

    for k in range(n_fills):
        pl.when(slot_ref[k] < n_slots)(lambda k=k: fill_copy(k).start())
    for index in range(n_slots):
        pl.when(kept(index))(lambda index=index: cache_copy(index).start())
    for index in range(n_slots):
        pl.when(kept(index))(lambda index=index: cache_copy(index).wait())
    for k in range(n_fills):
        pl.when(slot_ref[k] < n_slots)(lambda k=k: fill_copy(k).wait())


def fill(cache_rows, fills, miss_slot, fill_block):
    n_sems = cache_rows.shape[0] // BLOCK + miss_slot.shape[0]
    return pl.pallas_call(
        fill_kernel,
        out_shape=pltpu.VMEM(cache_rows.shape, cache_rows.dtype),
        in_specs=[SMEM_SPEC] * 2 + [ANY_SPEC] * 2,
        out_specs=VMEM_SPEC,
        scratch_shapes=[pltpu.SemaphoreType.DMA((n_sems,))],
        name="fill",
    )(miss_slot, fill_block, cache_rows, fills)


PICK = [1]


def gate_kernel(*refs):
    pass


def gate(arrays, after):
    n_arrays = len(arrays)
    if not arrays:
        return []
    return pl.pallas_call(
        gate_kernel,
        out_shape=[jax.ShapeDtypeStruct(one.shape, one.dtype) for one in arrays],
        in_specs=[ANY_SPEC] * (n_arrays + 1),
        out_specs=[ANY_SPEC] * n_arrays,
        input_output_aliases={index: index for index in range(n_arrays)},
        compiler_params=pltpu.CompilerParams(vmem_limit_bytes=1 << 20),
        name="gate",
    )(*arrays, after)


def pool_shards(first, rows, entry_refs, entry_held, shards, sems, held, table, sums):
    cap = entry_held[0].shape[0] // 8
    copies = [
        pltpu.make_async_copy(ref.at[pl.ds(first * cap, 8 * cap)], to, sems.at[len(shards) + index])
        for index, (ref, to) in enumerate(zip(entry_refs, entry_held))
    ]
    copies += [pltpu.make_async_copy(ref, held.at[s], sems.at[s]) for s, ref in enumerate(shards)]
    for copy in copies:
        copy.start()
    yield
    for copy in copies[:2]:
        copy.wait()
    slot_ref, bag_ref = entry_held
    for s, copy in enumerate(copies[2:]):
        copy.wait()
        table[...] = held[s].astype(jnp.float32)
        row = rows[s]

        def add_entries(step, _):
            start = row * cap + step * UNROLL
            for group in range(UNROLL // CHAINS):
                entries = [start + group * CHAINS + k for k in range(CHAINS)]
                slots = [slot_ref[e] for e in entries]
                bags = [bag_ref[e] for e in entries]
                found = [table[pl.ds(slot, 1), :] for slot in slots]
                olds = [sums[k][pl.ds(bags[k], 1), :] for k in range(CHAINS)]
                for k in range(CHAINS):
                    sums[k][pl.ds(bags[k], 1), :] = olds[k] + found[k]
            return 0

        lax.fori_loop(0, slot_ref[row * cap + cap - 1], add_entries, 0)


def pool_kernel(first, rows, is_first, slot_ref, bag_ref, *refs):
    shards, refs = refs[: len(rows)], refs[len(rows) :]
    if not is_first:
        refs = refs[CHAINS:]
    sums, (_, *entry_held, held, table, sems) = refs[:CHAINS], refs[CHAINS:]
    pooling = pool_shards(
        first, rows, (slot_ref, bag_ref), entry_held, shards, sems, held, table, sums
    )
    next(pooling)
    if is_first:
        for one in sums:
            one[...] = jnp.zeros_like(one)
    for _ in pooling:
        pass


def interact(sums, dense_ref, masked, queries):
    lane = lax.broadcasted_iota(jnp.int32, (8, 256), 1)
    row = lax.broadcasted_iota(jnp.int32, (8, 256), 0)
    own_query = (lane & 7) == row

    def sixteen_queries(step, _):
        dense = dense_ref[pl.ds(pl.multiple_of(step * 16, 16), 16), :].astype(jnp.float32)
        halves = []
        for half in range(2):
            query = pl.multiple_of(step * 16 + half * 8, 8)
            vectors = [dense[half * 8 : half * 8 + 8]]
            for feature in range(F):
                rows = pl.ds(pl.multiple_of(feature * queries + query, 8), 8)
                total = sums[0][rows, :]
                for one in sums[1:]:
                    total = total + one[rows, :]
                vectors.append(total)
            vectors += [jnp.zeros((8, LANES), jnp.float32)] * (32 - VECS)
            stacked = jnp.concatenate(vectors, axis=0).astype(jnp.bfloat16)
            halves.append(
                lax.dot_general(
                    stacked, stacked, (((1,), (1,)), ((), ())), preferred_element_type=jnp.float32
                )
            )
        for i in range(F):
            pair = [
                jnp.where(own_query, products[8 * i : 8 * i + 8, :], 0.0) for products in halves
            ]
            masked[i, pl.ds(pl.multiple_of(step * 16, 16), 16), :] = jnp.concatenate(
                pair, axis=0
            ).astype(jnp.bfloat16)
        return 0

    lax.fori_loop(0, queries // 16, sixteen_queries, 0, unroll=4)


def inter_columns(masked, dense_ref, inter, queries):
    spread = lax.broadcasted_iota(jnp.int32, (256, LANES), 0) // 8
    vector = lax.broadcasted_iota(jnp.int32, (256, LANES), 1)
    pick = jnp.where(spread == vector, 1.0, 0.0).astype(jnp.bfloat16)
    lane = lax.broadcasted_iota(jnp.int32, (queries, LANES), 1)
    tiles = [jnp.zeros((queries, LANES), jnp.float32) for _ in range(3)]
    first = 0
    for i in range(F):
        length = F - i
        picked = jnp.dot(masked[i], pick, preferred_element_type=jnp.float32)
        shift = (first - (i + 1)) % LANES
        if shift:
            picked = pltpu.roll(picked, shift, 1)
        for tile in range(3):
            low, high = max(first, tile * LANES), min(first + length, (tile + 1) * LANES)
            if low < high:
                inside = jnp.logical_and(lane >= low - tile * LANES, lane < high - tile * LANES)
                tiles[tile] = jnp.where(inside, picked, tiles[tile])
        first += length
    inter[:, :LANES] = dense_ref[...]
    for tile in range(3):
        inter[:, (tile + 1) * LANES : (tile + 2) * LANES] = tiles[tile].astype(jnp.bfloat16)


def final_kernel(first, n_shards, with_head, slot_ref, bag_ref, *refs):
    shards, refs = refs[:n_shards], refs[n_shards:]
    old_sums, dense_ref, refs = refs[:CHAINS], refs[CHAINS], refs[CHAINS + 1 :]
    if with_head:
        w_first, w_second, w_out, logits, *refs = refs
    else:
        inter, *refs = refs
    refs = refs[CHAINS:]
    if with_head:
        inter, first_held, second_held, weight_sems, *refs = refs
        weights = [
            pltpu.make_async_copy(w_first, first_held, weight_sems.at[0]),
            pltpu.make_async_copy(w_second, second_held, weight_sems.at[1]),
        ]
        for copy in weights:
            copy.start()
    masked, *entry_held, held, table, sems = refs
    queries = dense_ref.shape[0]
    for _ in pool_shards(
        first, (0, 1), (slot_ref, bag_ref), entry_held, shards, sems, held, table, old_sums
    ):
        pass
    interact(old_sums, dense_ref, masked, queries)
    inter_columns(masked, dense_ref, inter, queries)
    if not with_head:
        return
    for copy in weights:
        copy.wait()
    step = LANES
    inputs = first_held.shape[0]
    for part in range(queries // step):
        rows = slice(part * step, (part + 1) * step)
        hidden = jnp.dot(inter[rows, :inputs], first_held[...], preferred_element_type=jnp.float32)
        hidden = jnp.maximum(hidden, 0.0).astype(jnp.bfloat16)
        second = jnp.dot(hidden, second_held[...], preferred_element_type=jnp.float32)
        scored = jnp.maximum(second, 0.0) * w_out[...]
        folded = scored[:, :LANES]
        for tile in range(1, scored.shape[1] // LANES):
            folded = folded + scored[:, tile * LANES : (tile + 1) * LANES]
        logits[rows] = jnp.sum(folded.T, axis=0)


def pool_scratch(n_shards, shard_rows, cap):
    return [
        pltpu.SMEM((8 * cap,), jnp.int32),
        pltpu.SMEM((8 * cap,), jnp.int32),
        pltpu.VMEM((n_shards, shard_rows, LANES), jnp.bfloat16),
        pltpu.VMEM((shard_rows, LANES), jnp.float32),
        pltpu.SemaphoreType.DMA((n_shards + 2,)),
    ]


def pool(first, entries, cap, shards, sums, sum_rows, rows=(0, 1)):
    n_shards = len(shards)
    is_first = sums is None
    sums = [] if is_first else sums
    *sums, done = pl.pallas_call(
        functools.partial(pool_kernel, first, rows, is_first),
        out_shape=[pltpu.VMEM((sum_rows, LANES), jnp.float32)] * CHAINS
        + [jax.ShapeDtypeStruct((8, LANES), jnp.int32)],
        in_specs=[HBM_SPEC] * 2 + [ANY_SPEC] * n_shards + [VMEM_SPEC] * len(sums),
        out_specs=[VMEM_SPEC] * CHAINS + [ANY_SPEC],
        input_output_aliases={2 + n_shards + k: k for k in range(len(sums))},
        scratch_shapes=pool_scratch(n_shards, shards[0].shape[0], cap),
        compiler_params=pltpu.CompilerParams(vmem_limit_bytes=VMEM),
        cost_estimate=pl.CostEstimate(flops=0, bytes_accessed=n_shards * 3000000, transcendentals=0),
        name="pool",
    )(*entries, *shards, *sums)
    return sums, done


def finish(first, entries, cap, shards, sums, dense_rows, head):
    n_shards = len(shards)
    queries = dense_rows.shape[0]
    width = 4 * LANES
    masked = pltpu.VMEM((F, queries, 256), jnp.bfloat16)
    if head is None:
        head_args, head_specs = [], []
        out_shape = jax.ShapeDtypeStruct((queries, width), jnp.bfloat16)
        scratch = [masked]
    else:
        head_args, head_specs = list(head), [HBM_SPEC, HBM_SPEC, VMEM_SPEC]
        out_shape = jax.ShapeDtypeStruct((queries,), jnp.float32)
        scratch = [
            pltpu.VMEM((queries, width), jnp.bfloat16),
            pltpu.VMEM(head[0].shape, jnp.bfloat16),
            pltpu.VMEM(head[1].shape, jnp.bfloat16),
            pltpu.SemaphoreType.DMA((2,)),
            masked,
        ]
    out = pl.pallas_call(
        functools.partial(final_kernel, first, n_shards, head is not None),
        out_shape=[out_shape] + [pltpu.VMEM(one.shape, one.dtype) for one in sums],
        in_specs=[HBM_SPEC] * 2 + [ANY_SPEC] * n_shards + [VMEM_SPEC] * (CHAINS + 1) + head_specs,
        out_specs=[VMEM_SPEC] * (CHAINS + 1),
        input_output_aliases={2 + n_shards + k: 1 + k for k in range(CHAINS)},
        scratch_shapes=scratch + pool_scratch(n_shards, shards[0].shape[0], cap),
        compiler_params=pltpu.CompilerParams(vmem_limit_bytes=VMEM),
        name="finish",
    )(*entries, *shards, *sums, dense_rows, *head_args)
    return out[0]


def per_device(
    n_planes,
    cache_rows,
    store_rows,
    miss_block,
    miss_slot,
    lookup_slot,
    lookup_bag,
    dense_rows,
    w_first,
    w_second,
    w_out,
):
    emb_width = cache_rows.shape[1]
    queries = dense_rows.shape[0]
    bags = queries * F
    owners = lax.axis_size("owner")
    n_shards = n_planes * 8

    if owners == 1:
        fills, fill_block = store_rows, miss_block[0]
    else:
        fills = store_rows.reshape(-1, BLOCK, emb_width)[miss_block[0]]
        fills = lax.all_gather(fills, "owner", axis=0, tiled=True)
        fill_block = jnp.arange(fills.shape[0], dtype=jnp.int32)
        fills = fills.reshape(-1, emb_width)
    own = fill(cache_rows, fills, miss_slot[0], fill_block)

    def device(z, y, x, core):
        return ((z * 2 + y) * 2 + x) * 2 + core

    def hop(move):
        pairs = []
        for index in range(n_shards):
            at = (index // 8, index // 4 % 2, index // 2 % 2, index % 2)
            pairs.append((index, device(*move(*at))))
        return lambda array: lax.ppermute(array, "cache", pairs)

    next_plane = hop(lambda z, y, x, core: ((z + 1) % n_planes, y, x, core))
    first_hop = hop(lambda z, y, x, core: (z, y, 1 - x, core) if core == 0 else (z, 1 - y, x, core))
    second_hop = hop(lambda z, y, x, core: (z, 1 - y, x, core) if core == 0 else (z, y, 1 - x, core))
    other_core = hop(lambda z, y, x, core: (z, y, x, 1 - core))

    me = lax.axis_index("cache")
    z, y, x, core = me // 8, me // 4 % 2, me // 2 % 2, me % 2

    def origin(shift, flip_first, flip_second, side):
        flip_x = jnp.where(side == 0, flip_first, flip_second)
        flip_y = jnp.where(side == 0, flip_second, flip_first)
        return device((z - shift) % n_planes, y ^ flip_y, x ^ flip_x, side)

    def both_cores(shift, *flips):
        return [origin(shift, *flips, side) for side in (core, 1 - core)]

    unused = [0] * 6
    order = both_cores(0, 0, 0) + unused
    for shift in range(n_planes):
        before, after = max(shift - 1, 0), min(shift + 1, n_planes - 1)
        order += both_cores(shift, 1, 0) + both_cores(shift, 0, 1)
        order += both_cores(before, 1, 1) + both_cores(after, 0, 0)
    order += both_cores(n_planes - 1, 1, 1) + unused
    order = jnp.stack(order)
    cap = lookup_slot.shape[2]
    cap += -cap % LANES or LANES
    spare = ((0, 0), (0, cap - lookup_slot.shape[2]))
    slots = jnp.pad(lookup_slot[0], spare)[order]
    bag_ids = jnp.pad(lookup_bag[0], spare, constant_values=bags)[order]
    used = jnp.sum((bag_ids < bags).astype(jnp.int32), axis=1)
    steps = (used + UNROLL - 1) // UNROLL
    sum_rows = bags + 8
    places = jnp.where(bag_ids < bags, bag_ids % F * queries + bag_ids // F, bags)
    slots = jnp.where(jnp.arange(cap) == cap - 1, steps[:, None], slots)
    entries = (slots.reshape(-1), places.reshape(-1))

    def of_chip(array):
        return [array, other_core(array)]

    crossed, turned, next_piece = first_hop(own), second_hop(own), next_plane(own)
    sums, done = pool(0, entries, cap, of_chip(own), None, sum_rows)
    (crossed,) = gate([crossed], done)
    far = []
    for shift in range(n_planes):
        last = shift == n_planes - 1
        near = of_chip(crossed) + of_chip(turned)
        next_far = next_plane(far[0]) if shift == n_planes - 2 else second_hop(crossed)
        passed = [next_far]
        if not last:
            passed += [first_hop(next_piece), second_hop(next_piece)]
            piece = of_chip(next_piece)
            if shift < n_planes - 2:
                passed.append(next_plane(next_piece))
        else:
            piece = []
        if shift == 0:
            shards, rows = near + piece, [0, 1, 2, 3, 6, 7]
        else:
            shards, rows = near + far + piece, list(range(6 + len(piece)))
        sums, done = pool(8 * shift + 8, entries, cap, shards, sums, sum_rows, rows)
        chosen = [0] if last else [index for index in PICK if index < len(passed)]
        for index, one in zip(chosen, gate([passed[index] for index in chosen], done)):
            passed[index] = one
        next_far, *passed = passed
        far = of_chip(next_far)
        if not last:
            crossed, turned, *next_piece = passed
            next_piece = next_piece[0] if next_piece else None
    args = (8 * n_planes + 8, entries, cap, far, sums, dense_rows)
    if owners == 1:
        return finish(*args, (w_first, w_second, w_out.reshape(1, -1)))
    inter_in = finish(*args, None)[:, : w_first.shape[0]]
    group_inputs = lax.all_gather(inter_in, "owner", axis=0, tiled=True)
    hidden = jax.nn.relu(jnp.dot(group_inputs, w_first, preferred_element_type=jnp.float32))
    second = lax.psum_scatter(
        jnp.dot(hidden.astype(jnp.bfloat16), w_second, preferred_element_type=jnp.float32),
        "owner",
        scatter_dimension=0,
        tiled=True,
    )
    return jnp.sum(jax.nn.relu(second) * w_out, axis=1)


def solution(mesh):
    in_specs = (
        P(("rep", "cache"), None),
        P(("rep", "cache", "owner"), None),
        P(("rep", "cache", "owner"), None),
        P(("rep", "cache"), None),
        P(("rep", "cache", "owner"), None, None),
        P(("rep", "cache", "owner"), None, None),
        P(("rep", "cache", "owner"), None),
        P(None, "owner"),
        P("owner", None),
        P(),
    )
    out_specs = P(("rep", "cache", "owner"))
    return jax.shard_map(
        functools.partial(per_device, mesh.shape["cache"] // 8),
        mesh=mesh,
        in_specs=in_specs,
        out_specs=out_specs,
        check_vma=False,
    )
```

```python
import functools

import jax
import jax.numpy as jnp
from jax import lax
from jax.experimental import pallas as pl
from jax.experimental.pallas import tpu as pltpu
from jax.sharding import PartitionSpec as P

F = 26
BLOCK = 128
VECS = F + 1
LANES = 128
CHAINS = 4
UNROLL = 32
VMEM = 18 << 20
SMEM_SPEC = pl.BlockSpec(memory_space=pltpu.SMEM)
ANY_SPEC = pl.BlockSpec(memory_space=pl.ANY)
HBM_SPEC = pl.BlockSpec(memory_space=pltpu.HBM)
VMEM_SPEC = pl.BlockSpec(memory_space=pltpu.VMEM)


def fill_kernel(slot_ref, block_ref, cache_ref, fills_ref, out_ref, sem):
    def of_block(ref, index):
        return ref.at[pl.ds(pl.multiple_of(index * BLOCK, BLOCK), BLOCK)]

    n_slots = out_ref.shape[0] // BLOCK
    n_fills = slot_ref.shape[0]

    def kept(index):
        hit = slot_ref[0] == index
        for k in range(1, n_fills):
            hit = jnp.logical_or(hit, slot_ref[k] == index)
        return jnp.logical_not(hit)

    def cache_copy(index):
        return pltpu.make_async_copy(of_block(cache_ref, index), of_block(out_ref, index), sem.at[index])

    def fill_copy(k):
        slot = jnp.minimum(slot_ref[k], n_slots - 1)
        return pltpu.make_async_copy(
            of_block(fills_ref, block_ref[k]), of_block(out_ref, slot), sem.at[n_slots + k]
        )

    for k in range(n_fills):
        pl.when(slot_ref[k] < n_slots)(lambda k=k: fill_copy(k).start())
    for index in range(n_slots):
        pl.when(kept(index))(lambda index=index: cache_copy(index).start())
    for index in range(n_slots):
        pl.when(kept(index))(lambda index=index: cache_copy(index).wait())
    for k in range(n_fills):
        pl.when(slot_ref[k] < n_slots)(lambda k=k: fill_copy(k).wait())


def fill(cache_rows, fills, miss_slot, fill_block):
    n_sems = cache_rows.shape[0] // BLOCK + miss_slot.shape[0]
    return pl.pallas_call(
        fill_kernel,
        out_shape=pltpu.VMEM(cache_rows.shape, cache_rows.dtype),
        in_specs=[SMEM_SPEC] * 2 + [ANY_SPEC] * 2,
        out_specs=VMEM_SPEC,
        scratch_shapes=[pltpu.SemaphoreType.DMA((n_sems,))],
        name="fill",
    )(miss_slot, fill_block, cache_rows, fills)


PICK = [1]


def gate_kernel(*refs):
    pass


def gate(arrays, after):
    n_arrays = len(arrays)
    if not arrays:
        return []
    return pl.pallas_call(
        gate_kernel,
        out_shape=[jax.ShapeDtypeStruct(one.shape, one.dtype) for one in arrays],
        in_specs=[ANY_SPEC] * (n_arrays + 1),
        out_specs=[ANY_SPEC] * n_arrays,
        input_output_aliases={index: index for index in range(n_arrays)},
        compiler_params=pltpu.CompilerParams(vmem_limit_bytes=1 << 20),
        name="gate",
    )(*arrays, after)


def pool_shards(first, rows, entry_refs, entry_held, shards, sems, held, table, sums):
    cap = entry_held[0].shape[0] // 8
    copies = [
        pltpu.make_async_copy(ref.at[pl.ds(first * cap, 8 * cap)], to, sems.at[len(shards) + index])
        for index, (ref, to) in enumerate(zip(entry_refs, entry_held))
    ]
    copies += [pltpu.make_async_copy(ref, held.at[s], sems.at[s]) for s, ref in enumerate(shards)]
    for copy in copies:
        copy.start()
    yield
    for copy in copies[:2]:
        copy.wait()
    slot_ref, bag_ref = entry_held
    for s, copy in enumerate(copies[2:]):
        copy.wait()
        table[...] = held[s].astype(jnp.float32)
        row = rows[s]

        def add_entries(step, _):
            start = row * cap + step * UNROLL
            for group in range(UNROLL // CHAINS):
                entries = [start + group * CHAINS + k for k in range(CHAINS)]
                slots = [slot_ref[e] for e in entries]
                bags = [bag_ref[e] for e in entries]
                found = [table[pl.ds(slot, 1), :] for slot in slots]
                olds = [sums[k][pl.ds(bags[k], 1), :] for k in range(CHAINS)]
                for k in range(CHAINS):
                    sums[k][pl.ds(bags[k], 1), :] = olds[k] + found[k]
            return 0

        lax.fori_loop(0, slot_ref[row * cap + cap - 1], add_entries, 0)


def pool_kernel(first, rows, is_first, slot_ref, bag_ref, *refs):
    shards, refs = refs[: len(rows)], refs[len(rows) :]
    if not is_first:
        refs = refs[CHAINS:]
    sums, (_, *entry_held, held, table, sems) = refs[:CHAINS], refs[CHAINS:]
    pooling = pool_shards(
        first, rows, (slot_ref, bag_ref), entry_held, shards, sems, held, table, sums
    )
    next(pooling)
    if is_first:
        for one in sums:
            one[...] = jnp.zeros_like(one)
    for _ in pooling:
        pass


def interact(sums, dense_ref, masked, queries):
    lane = lax.broadcasted_iota(jnp.int32, (8, 256), 1)
    row = lax.broadcasted_iota(jnp.int32, (8, 256), 0)
    own_query = (lane & 7) == row

    def sixteen_queries(step, _):
        dense = dense_ref[pl.ds(pl.multiple_of(step * 16, 16), 16), :].astype(jnp.float32)
        halves = []
        for half in range(2):
            query = pl.multiple_of(step * 16 + half * 8, 8)
            vectors = [dense[half * 8 : half * 8 + 8]]
            for feature in range(F):
                rows = pl.ds(pl.multiple_of(feature * queries + query, 8), 8)
                total = sums[0][rows, :]
                for one in sums[1:]:
                    total = total + one[rows, :]
                vectors.append(total)
            vectors += [jnp.zeros((8, LANES), jnp.float32)] * (32 - VECS)
            stacked = jnp.concatenate(vectors, axis=0).astype(jnp.bfloat16)
            halves.append(
                lax.dot_general(
                    stacked, stacked, (((1,), (1,)), ((), ())), preferred_element_type=jnp.float32
                )
            )
        for i in range(F):
            pair = [
                jnp.where(own_query, products[8 * i : 8 * i + 8, :], 0.0) for products in halves
            ]
            masked[i, pl.ds(pl.multiple_of(step * 16, 16), 16), :] = jnp.concatenate(
                pair, axis=0
            ).astype(jnp.bfloat16)
        return 0

    lax.fori_loop(0, queries // 16, sixteen_queries, 0, unroll=8)


def inter_columns(masked, dense_ref, inter, queries):
    spread = lax.broadcasted_iota(jnp.int32, (256, LANES), 0) // 8
    vector = lax.broadcasted_iota(jnp.int32, (256, LANES), 1)
    pick = jnp.where(spread == vector, 1.0, 0.0).astype(jnp.bfloat16)
    lane = lax.broadcasted_iota(jnp.int32, (queries, LANES), 1)
    tiles = [jnp.zeros((queries, LANES), jnp.float32) for _ in range(3)]
    first = 0
    for i in range(F):
        length = F - i
        picked = jnp.dot(masked[i], pick, preferred_element_type=jnp.float32)
        shift = (first - (i + 1)) % LANES
        if shift:
            picked = pltpu.roll(picked, shift, 1)
        for tile in range(3):
            low, high = max(first, tile * LANES), min(first + length, (tile + 1) * LANES)
            if low < high:
                inside = jnp.logical_and(lane >= low - tile * LANES, lane < high - tile * LANES)
                tiles[tile] = jnp.where(inside, picked, tiles[tile])
        first += length
    inter[:, :LANES] = dense_ref[...]
    for tile in range(3):
        inter[:, (tile + 1) * LANES : (tile + 2) * LANES] = tiles[tile].astype(jnp.bfloat16)


def final_kernel(first, n_shards, with_head, slot_ref, bag_ref, *refs):
    shards, refs = refs[:n_shards], refs[n_shards:]
    old_sums, dense_ref, refs = refs[:CHAINS], refs[CHAINS], refs[CHAINS + 1 :]
    if with_head:
        w_first, w_second, w_out, logits, *refs = refs
    else:
        inter, *refs = refs
    refs = refs[CHAINS:]
    if with_head:
        inter, first_held, second_held, weight_sems, *refs = refs
        weights = [
            pltpu.make_async_copy(w_first, first_held, weight_sems.at[0]),
            pltpu.make_async_copy(w_second, second_held, weight_sems.at[1]),
        ]
        for copy in weights:
            copy.start()
    masked, *entry_held, held, table, sems = refs
    queries = dense_ref.shape[0]
    for _ in pool_shards(
        first, (0, 1), (slot_ref, bag_ref), entry_held, shards, sems, held, table, old_sums
    ):
        pass
    interact(old_sums, dense_ref, masked, queries)
    inter_columns(masked, dense_ref, inter, queries)
    if not with_head:
        return
    for copy in weights:
        copy.wait()
    step = LANES
    inputs = first_held.shape[0]
    for part in range(queries // step):
        rows = slice(part * step, (part + 1) * step)
        hidden = jnp.dot(inter[rows, :inputs], first_held[...], preferred_element_type=jnp.float32)
        hidden = jnp.maximum(hidden, 0.0).astype(jnp.bfloat16)
        second = jnp.dot(hidden, second_held[...], preferred_element_type=jnp.float32)
        scored = jnp.maximum(second, 0.0) * w_out[...]
        folded = scored[:, :LANES]
        for tile in range(1, scored.shape[1] // LANES):
            folded = folded + scored[:, tile * LANES : (tile + 1) * LANES]
        logits[rows] = jnp.sum(folded.T, axis=0)


def pool_scratch(n_shards, shard_rows, cap):
    return [
        pltpu.SMEM((8 * cap,), jnp.int32),
        pltpu.SMEM((8 * cap,), jnp.int32),
        pltpu.VMEM((n_shards, shard_rows, LANES), jnp.bfloat16),
        pltpu.VMEM((shard_rows, LANES), jnp.float32),
        pltpu.SemaphoreType.DMA((n_shards + 2,)),
    ]


def pool(first, entries, cap, shards, sums, sum_rows, rows=(0, 1)):
    n_shards = len(shards)
    is_first = sums is None
    sums = [] if is_first else sums
    *sums, done = pl.pallas_call(
        functools.partial(pool_kernel, first, rows, is_first),
        out_shape=[pltpu.VMEM((sum_rows, LANES), jnp.float32)] * CHAINS
        + [jax.ShapeDtypeStruct((8, LANES), jnp.int32)],
        in_specs=[HBM_SPEC] * 2 + [ANY_SPEC] * n_shards + [VMEM_SPEC] * len(sums),
        out_specs=[VMEM_SPEC] * CHAINS + [ANY_SPEC],
        input_output_aliases={2 + n_shards + k: k for k in range(len(sums))},
        scratch_shapes=pool_scratch(n_shards, shards[0].shape[0], cap),
        compiler_params=pltpu.CompilerParams(vmem_limit_bytes=VMEM),
        cost_estimate=pl.CostEstimate(flops=0, bytes_accessed=n_shards * 3000000, transcendentals=0),
        name="pool",
    )(*entries, *shards, *sums)
    return sums, done


def finish(first, entries, cap, shards, sums, dense_rows, head):
    n_shards = len(shards)
    queries = dense_rows.shape[0]
    width = 4 * LANES
    masked = pltpu.VMEM((F, queries, 256), jnp.bfloat16)
    if head is None:
        head_args, head_specs = [], []
        out_shape = jax.ShapeDtypeStruct((queries, width), jnp.bfloat16)
        scratch = [masked]
    else:
        head_args, head_specs = list(head), [HBM_SPEC, HBM_SPEC, VMEM_SPEC]
        out_shape = jax.ShapeDtypeStruct((queries,), jnp.float32)
        scratch = [
            pltpu.VMEM((queries, width), jnp.bfloat16),
            pltpu.VMEM(head[0].shape, jnp.bfloat16),
            pltpu.VMEM(head[1].shape, jnp.bfloat16),
            pltpu.SemaphoreType.DMA((2,)),
            masked,
        ]
    out = pl.pallas_call(
        functools.partial(final_kernel, first, n_shards, head is not None),
        out_shape=[out_shape] + [pltpu.VMEM(one.shape, one.dtype) for one in sums],
        in_specs=[HBM_SPEC] * 2 + [ANY_SPEC] * n_shards + [VMEM_SPEC] * (CHAINS + 1) + head_specs,
        out_specs=[VMEM_SPEC] * (CHAINS + 1),
        input_output_aliases={2 + n_shards + k: 1 + k for k in range(CHAINS)},
        scratch_shapes=scratch + pool_scratch(n_shards, shards[0].shape[0], cap),
        compiler_params=pltpu.CompilerParams(vmem_limit_bytes=VMEM),
        name="finish",
    )(*entries, *shards, *sums, dense_rows, *head_args)
    return out[0]


def per_device(
    n_planes,
    cache_rows,
    store_rows,
    miss_block,
    miss_slot,
    lookup_slot,
    lookup_bag,
    dense_rows,
    w_first,
    w_second,
    w_out,
):
    emb_width = cache_rows.shape[1]
    queries = dense_rows.shape[0]
    bags = queries * F
    owners = lax.axis_size("owner")
    n_shards = n_planes * 8

    if owners == 1:
        fills, fill_block = store_rows, miss_block[0]
    else:
        fills = store_rows.reshape(-1, BLOCK, emb_width)[miss_block[0]]
        fills = lax.all_gather(fills, "owner", axis=0, tiled=True)
        fill_block = jnp.arange(fills.shape[0], dtype=jnp.int32)
        fills = fills.reshape(-1, emb_width)
    own = fill(cache_rows, fills, miss_slot[0], fill_block)

    def device(z, y, x, core):
        return ((z * 2 + y) * 2 + x) * 2 + core

    def hop(move):
        pairs = []
        for index in range(n_shards):
            at = (index // 8, index // 4 % 2, index // 2 % 2, index % 2)
            pairs.append((index, device(*move(*at))))
        return lambda array: lax.ppermute(array, "cache", pairs)

    next_plane = hop(lambda z, y, x, core: ((z + 1) % n_planes, y, x, core))
    first_hop = hop(lambda z, y, x, core: (z, y, 1 - x, core) if core == 0 else (z, 1 - y, x, core))
    second_hop = hop(lambda z, y, x, core: (z, 1 - y, x, core) if core == 0 else (z, y, 1 - x, core))
    other_core = hop(lambda z, y, x, core: (z, y, x, 1 - core))

    me = lax.axis_index("cache")
    z, y, x, core = me // 8, me // 4 % 2, me // 2 % 2, me % 2

    def origin(shift, flip_first, flip_second, side):
        flip_x = jnp.where(side == 0, flip_first, flip_second)
        flip_y = jnp.where(side == 0, flip_second, flip_first)
        return device((z - shift) % n_planes, y ^ flip_y, x ^ flip_x, side)

    def both_cores(shift, *flips):
        return [origin(shift, *flips, side) for side in (core, 1 - core)]

    unused = [0] * 6
    order = both_cores(0, 0, 0) + unused
    for shift in range(n_planes):
        before, after = max(shift - 1, 0), min(shift + 1, n_planes - 1)
        order += both_cores(shift, 1, 0)
        order += [both_cores(shift, 0, 1)[0], both_cores(before, 0, min(shift, 1))[1]]
        order += both_cores(before, 1, 1)
        order += both_cores(after, 0, 0) if after > shift else [both_cores(shift, 0, 1)[1], 0]
    order += both_cores(n_planes - 1, 1, 1) + unused
    order = jnp.stack(order)
    cap = lookup_slot.shape[2]
    cap += -cap % LANES or LANES
    spare = ((0, 0), (0, cap - lookup_slot.shape[2]))
    slots = jnp.pad(lookup_slot[0], spare)[order]
    bag_ids = jnp.pad(lookup_bag[0], spare, constant_values=bags)[order]
    used = jnp.sum((bag_ids < bags).astype(jnp.int32), axis=1)
    steps = (used + UNROLL - 1) // UNROLL
    sum_rows = bags + 8
    places = jnp.where(bag_ids < bags, bag_ids % F * queries + bag_ids // F, bags)
    slots = jnp.where(jnp.arange(cap) == cap - 1, steps[:, None], slots)
    entries = (slots.reshape(-1), places.reshape(-1))

    def of_chip(array):
        return [array, other_core(array)]

    crossed, turned, next_piece = first_hop(own), second_hop(own), next_plane(own)
    sums, done = pool(0, entries, cap, [own], None, sum_rows, [0])
    (crossed,) = gate([crossed], done)
    far, late = [], other_core(own)
    for shift in range(n_planes):
        last = shift == n_planes - 1
        near = of_chip(crossed) + [turned]
        other_turned = other_core(turned)
        next_far = next_plane(far[0]) if shift == n_planes - 2 else second_hop(crossed)
        passed = [next_far]
        if not last:
            passed += [first_hop(next_piece), second_hop(next_piece)]
            piece = of_chip(next_piece)
            if shift < n_planes - 2:
                passed.append(next_plane(next_piece))
        else:
            piece = [other_turned]
        if shift == 0:
            shards, rows = near + [late] + piece, [0, 1, 2, 3, 6, 7]
        else:
            shards, rows = near + [late] + far + piece, list(range(6 + len(piece)))
        sums, done = pool(8 * shift + 8, entries, cap, shards, sums, sum_rows, rows)
        chosen = [0] if last else [1, 0] if shift == n_planes - 2 else [index for index in PICK if index < len(passed)]
        for index, one in zip(chosen, gate([passed[index] for index in chosen], done)):
            passed[index] = one
        next_far, *passed = passed
        far, late = of_chip(next_far), other_turned
        if not last:
            crossed, turned, *next_piece = passed
            next_piece = next_piece[0] if next_piece else None
    args = (8 * n_planes + 8, entries, cap, far, sums, dense_rows)
    if owners == 1:
        return finish(*args, (w_first, w_second, w_out.reshape(1, -1)))
    inter_in = finish(*args, None)[:, : w_first.shape[0]]
    group_inputs = lax.all_gather(inter_in, "owner", axis=0, tiled=True)
    hidden = jax.nn.relu(jnp.dot(group_inputs, w_first, preferred_element_type=jnp.float32))
    second = lax.psum_scatter(
        jnp.dot(hidden.astype(jnp.bfloat16), w_second, preferred_element_type=jnp.float32),
        "owner",
        scatter_dimension=0,
        tiled=True,
    )
    return jnp.sum(jax.nn.relu(second) * w_out, axis=1)


def solution(mesh):
    in_specs = (
        P(("rep", "cache"), None),
        P(("rep", "cache", "owner"), None),
        P(("rep", "cache", "owner"), None),
        P(("rep", "cache"), None),
        P(("rep", "cache", "owner"), None, None),
        P(("rep", "cache", "owner"), None, None),
        P(("rep", "cache", "owner"), None),
        P(None, "owner"),
        P("owner", None),
        P(),
    )
    out_specs = P(("rep", "cache", "owner"))
    return jax.shard_map(
        functools.partial(per_device, mesh.shape["cache"] // 8),
        mesh=mesh,
        in_specs=in_specs,
        out_specs=out_specs,
        check_vma=False,
    )
```

```python
import functools

import jax
import jax.numpy as jnp
from jax import lax
from jax.experimental import pallas as pl
from jax.experimental.pallas import tpu as pltpu
from jax.sharding import PartitionSpec as P

F = 26
BLOCK = 128
VECS = F + 1
LANES = 128
CHAINS = 4
UNROLL = 32
VMEM = 18 << 20
SMEM_SPEC = pl.BlockSpec(memory_space=pltpu.SMEM)
ANY_SPEC = pl.BlockSpec(memory_space=pl.ANY)
HBM_SPEC = pl.BlockSpec(memory_space=pltpu.HBM)
VMEM_SPEC = pl.BlockSpec(memory_space=pltpu.VMEM)


def fill_kernel(slot_ref, block_ref, cache_ref, fills_ref, out_ref, sem):
    def of_block(ref, index):
        return ref.at[pl.ds(pl.multiple_of(index * BLOCK, BLOCK), BLOCK)]

    n_slots = out_ref.shape[0] // BLOCK
    n_fills = slot_ref.shape[0]

    def kept(index):
        hit = slot_ref[0] == index
        for k in range(1, n_fills):
            hit = jnp.logical_or(hit, slot_ref[k] == index)
        return jnp.logical_not(hit)

    def cache_copy(index):
        return pltpu.make_async_copy(of_block(cache_ref, index), of_block(out_ref, index), sem.at[index])

    def fill_copy(k):
        slot = jnp.minimum(slot_ref[k], n_slots - 1)
        return pltpu.make_async_copy(
            of_block(fills_ref, block_ref[k]), of_block(out_ref, slot), sem.at[n_slots + k]
        )

    for k in range(n_fills):
        pl.when(slot_ref[k] < n_slots)(lambda k=k: fill_copy(k).start())
    for index in range(n_slots):
        pl.when(kept(index))(lambda index=index: cache_copy(index).start())
    for index in range(n_slots):
        pl.when(kept(index))(lambda index=index: cache_copy(index).wait())
    for k in range(n_fills):
        pl.when(slot_ref[k] < n_slots)(lambda k=k: fill_copy(k).wait())


def fill(cache_rows, fills, miss_slot, fill_block):
    n_sems = cache_rows.shape[0] // BLOCK + miss_slot.shape[0]
    return pl.pallas_call(
        fill_kernel,
        out_shape=pltpu.VMEM(cache_rows.shape, cache_rows.dtype),
        in_specs=[SMEM_SPEC] * 2 + [ANY_SPEC] * 2,
        out_specs=VMEM_SPEC,
        scratch_shapes=[pltpu.SemaphoreType.DMA((n_sems,))],
        name="fill",
    )(miss_slot, fill_block, cache_rows, fills)


PICK = [1]


def gate_kernel(*refs):
    pass


def gate(arrays, after):
    n_arrays = len(arrays)
    if not arrays:
        return []
    return pl.pallas_call(
        gate_kernel,
        out_shape=[jax.ShapeDtypeStruct(one.shape, one.dtype) for one in arrays],
        in_specs=[ANY_SPEC] * (n_arrays + 1),
        out_specs=[ANY_SPEC] * n_arrays,
        input_output_aliases={index: index for index in range(n_arrays)},
        compiler_params=pltpu.CompilerParams(vmem_limit_bytes=1 << 20),
        name="gate",
    )(*arrays, after)


def pool_shards(first, rows, entry_refs, entry_held, shards, sems, held, table, sums):
    cap = entry_held[0].shape[0] // 8
    copies = [
        pltpu.make_async_copy(ref.at[pl.ds(first * cap, 8 * cap)], to, sems.at[len(shards) + index])
        for index, (ref, to) in enumerate(zip(entry_refs, entry_held))
    ]
    copies += [pltpu.make_async_copy(ref, held.at[s], sems.at[s]) for s, ref in enumerate(shards)]
    for copy in copies:
        copy.start()
    yield
    for copy in copies[:2]:
        copy.wait()
    slot_ref, bag_ref = entry_held
    for s, copy in enumerate(copies[2:]):
        copy.wait()
        table[...] = held[s].astype(jnp.float32)
        row = rows[s]

        def add_entries(step, _):
            start = row * cap + step * UNROLL
            for group in range(UNROLL // CHAINS):
                entries = [start + group * CHAINS + k for k in range(CHAINS)]
                slots = [slot_ref[e] for e in entries]
                bags = [bag_ref[e] for e in entries]
                found = [table[pl.ds(slot, 1), :] for slot in slots]
                olds = [sums[k][pl.ds(bags[k], 1), :] for k in range(CHAINS)]
                for k in range(CHAINS):
                    sums[k][pl.ds(bags[k], 1), :] = olds[k] + found[k]
            return 0

        lax.fori_loop(0, slot_ref[row * cap + cap - 1], add_entries, 0)


def pool_kernel(first, rows, is_first, slot_ref, bag_ref, *refs):
    shards, refs = refs[: len(rows)], refs[len(rows) :]
    if not is_first:
        refs = refs[CHAINS:]
    sums, (_, *entry_held, held, table, sems) = refs[:CHAINS], refs[CHAINS:]
    pooling = pool_shards(
        first, rows, (slot_ref, bag_ref), entry_held, shards, sems, held, table, sums
    )
    next(pooling)
    if is_first:
        for one in sums:
            one[...] = jnp.zeros_like(one)
    for _ in pooling:
        pass


def interact(sums, dense_ref, masked, queries):
    lane = lax.broadcasted_iota(jnp.int32, (8, 256), 1)
    row = lax.broadcasted_iota(jnp.int32, (8, 256), 0)
    own_query = (lane & 7) == row

    def sixteen_queries(step, _):
        dense = dense_ref[pl.ds(pl.multiple_of(step * 16, 16), 16), :].astype(jnp.float32)
        halves = []
        for half in range(2):
            query = pl.multiple_of(step * 16 + half * 8, 8)
            vectors = [dense[half * 8 : half * 8 + 8]]
            for feature in range(F):
                rows = pl.ds(pl.multiple_of(feature * queries + query, 8), 8)
                total = sums[0][rows, :]
                for one in sums[1:]:
                    total = total + one[rows, :]
                vectors.append(total)
            vectors += [jnp.zeros((8, LANES), jnp.float32)] * (32 - VECS)
            stacked = jnp.concatenate(vectors, axis=0).astype(jnp.bfloat16)
            halves.append(
                lax.dot_general(
                    stacked[: 8 * F], stacked, (((1,), (1,)), ((), ())), preferred_element_type=jnp.float32
                )
            )
        for i in range(F):
            pair = [
                jnp.where(own_query, products[8 * i : 8 * i + 8, :], 0.0) for products in halves
            ]
            masked[i, pl.ds(pl.multiple_of(step * 16, 16), 16), :] = jnp.concatenate(
                pair, axis=0
            ).astype(jnp.bfloat16)
        return 0

    lax.fori_loop(0, queries // 16, sixteen_queries, 0, unroll=12)


def inter_columns(masked, dense_ref, inter, queries):
    spread = lax.broadcasted_iota(jnp.int32, (256, LANES), 0) // 8
    vector = lax.broadcasted_iota(jnp.int32, (256, LANES), 1)
    pick = jnp.where(spread == vector, 1.0, 0.0).astype(jnp.bfloat16)
    lane = lax.broadcasted_iota(jnp.int32, (queries, LANES), 1)
    tiles = [jnp.zeros((queries, LANES), jnp.float32) for _ in range(3)]
    first = 0
    for i in range(F):
        length = F - i
        picked = jnp.dot(masked[i], pick, preferred_element_type=jnp.float32)
        shift = (first - (i + 1)) % LANES
        if shift:
            picked = pltpu.roll(picked, shift, 1)
        for tile in range(3):
            low, high = max(first, tile * LANES), min(first + length, (tile + 1) * LANES)
            if low < high:
                inside = jnp.logical_and(lane >= low - tile * LANES, lane < high - tile * LANES)
                tiles[tile] = jnp.where(inside, picked, tiles[tile])
        first += length
    inter[:, :LANES] = dense_ref[...]
    for tile in range(3):
        inter[:, (tile + 1) * LANES : (tile + 2) * LANES] = tiles[tile].astype(jnp.bfloat16)


def final_kernel(first, n_shards, with_head, slot_ref, bag_ref, *refs):
    shards, refs = refs[:n_shards], refs[n_shards:]
    old_sums, dense_ref, refs = refs[:CHAINS], refs[CHAINS], refs[CHAINS + 1 :]
    if with_head:
        w_first, w_second, w_out, logits, *refs = refs
    else:
        inter, *refs = refs
    refs = refs[CHAINS:]
    if with_head:
        inter, first_held, second_held, out_held, weight_sems, *refs = refs
    masked, dense_held, dense_sem, *entry_held, held, table, sems = refs
    queries = dense_ref.shape[0]
    pooling = pool_shards(
        first, (0, 1), (slot_ref, bag_ref), entry_held, shards, sems, held, table, old_sums
    )
    next(pooling)
    dense_copy = pltpu.make_async_copy(dense_ref, dense_held, dense_sem)
    dense_copy.start()
    if with_head:
        weights = [
            pltpu.make_async_copy(w_first, first_held, weight_sems.at[0]),
            pltpu.make_async_copy(w_second, second_held, weight_sems.at[1]),
            pltpu.make_async_copy(w_out, out_held, weight_sems.at[2]),
        ]
        for copy in weights:
            copy.start()
    for _ in pooling:
        pass
    dense_copy.wait()
    interact(old_sums, dense_held, masked, queries)
    inter_columns(masked, dense_held, inter, queries)
    if not with_head:
        return
    for copy in weights:
        copy.wait()
    step = LANES
    inputs = first_held.shape[0]
    for part in range(queries // step):
        rows = slice(part * step, (part + 1) * step)
        hidden = jnp.dot(inter[rows, :inputs], first_held[...], preferred_element_type=jnp.float32)
        hidden = jnp.maximum(hidden, 0.0).astype(jnp.bfloat16)
        second = jnp.dot(hidden, second_held[...], preferred_element_type=jnp.float32)
        scored = jnp.maximum(second, 0.0) * out_held[...]
        folded = scored[:, :LANES]
        for tile in range(1, scored.shape[1] // LANES):
            folded = folded + scored[:, tile * LANES : (tile + 1) * LANES]
        logits[rows] = jnp.sum(folded.T, axis=0)


def pool_scratch(n_shards, shard_rows, cap):
    return [
        pltpu.SMEM((8 * cap,), jnp.int32),
        pltpu.SMEM((8 * cap,), jnp.int32),
        pltpu.VMEM((n_shards, shard_rows, LANES), jnp.bfloat16),
        pltpu.VMEM((shard_rows, LANES), jnp.float32),
        pltpu.SemaphoreType.DMA((n_shards + 2,)),
    ]


def pool(first, entries, cap, shards, sums, sum_rows, rows=(0, 1)):
    n_shards = len(shards)
    is_first = sums is None
    sums = [] if is_first else sums
    *sums, done = pl.pallas_call(
        functools.partial(pool_kernel, first, rows, is_first),
        out_shape=[pltpu.VMEM((sum_rows, LANES), jnp.float32)] * CHAINS
        + [jax.ShapeDtypeStruct((8, LANES), jnp.int32)],
        in_specs=[HBM_SPEC] * 2 + [ANY_SPEC] * n_shards + [VMEM_SPEC] * len(sums),
        out_specs=[VMEM_SPEC] * CHAINS + [ANY_SPEC],
        input_output_aliases={2 + n_shards + k: k for k in range(len(sums))},
        scratch_shapes=pool_scratch(n_shards, shards[0].shape[0], cap),
        compiler_params=pltpu.CompilerParams(vmem_limit_bytes=VMEM),
        cost_estimate=pl.CostEstimate(flops=0, bytes_accessed=n_shards * 3000000, transcendentals=0),
        name="pool",
    )(*entries, *shards, *sums)
    return sums, done


def finish(first, entries, cap, shards, sums, dense_rows, head):
    n_shards = len(shards)
    queries = dense_rows.shape[0]
    width = 4 * LANES
    masked = [
        pltpu.VMEM((F, queries, 256), jnp.bfloat16),
        pltpu.VMEM(dense_rows.shape, dense_rows.dtype),
        pltpu.SemaphoreType.DMA,
    ]
    if head is None:
        head_args, head_specs = [], []
        out_shape = jax.ShapeDtypeStruct((queries, width), jnp.bfloat16)
        scratch = masked
    else:
        head_args, head_specs = list(head), [HBM_SPEC, HBM_SPEC, ANY_SPEC]
        out_shape = jax.ShapeDtypeStruct((queries,), jnp.float32)
        scratch = [
            pltpu.VMEM((queries, width), jnp.bfloat16),
            pltpu.VMEM(head[0].shape, jnp.bfloat16),
            pltpu.VMEM(head[1].shape, jnp.bfloat16),
            pltpu.VMEM(head[2].shape, jnp.float32),
            pltpu.SemaphoreType.DMA((3,)),
            *masked,
        ]
    out = pl.pallas_call(
        functools.partial(final_kernel, first, n_shards, head is not None),
        out_shape=[out_shape] + [pltpu.VMEM(one.shape, one.dtype) for one in sums],
        in_specs=[HBM_SPEC] * 2 + [ANY_SPEC] * n_shards + [VMEM_SPEC] * CHAINS + [ANY_SPEC] + head_specs,
        out_specs=[VMEM_SPEC] * (CHAINS + 1),
        input_output_aliases={2 + n_shards + k: 1 + k for k in range(CHAINS)},
        scratch_shapes=scratch + pool_scratch(n_shards, shards[0].shape[0], cap),
        compiler_params=pltpu.CompilerParams(vmem_limit_bytes=VMEM),
        name="finish",
    )(*entries, *shards, *sums, dense_rows, *head_args)
    return out[0]


def per_device(
    n_planes,
    cache_rows,
    store_rows,
    miss_block,
    miss_slot,
    lookup_slot,
    lookup_bag,
    dense_rows,
    w_first,
    w_second,
    w_out,
):
    emb_width = cache_rows.shape[1]
    queries = dense_rows.shape[0]
    bags = queries * F
    owners = lax.axis_size("owner")
    n_shards = n_planes * 8

    if owners == 1:
        fills, fill_block = store_rows, miss_block[0]
    else:
        fills = store_rows.reshape(-1, BLOCK, emb_width)[miss_block[0]]
        fills = lax.all_gather(fills, "owner", axis=0, tiled=True)
        fill_block = jnp.arange(fills.shape[0], dtype=jnp.int32)
        fills = fills.reshape(-1, emb_width)
    own = fill(cache_rows, fills, miss_slot[0], fill_block)

    def device(z, y, x, core):
        return ((z * 2 + y) * 2 + x) * 2 + core

    def hop(move):
        pairs = []
        for index in range(n_shards):
            at = (index // 8, index // 4 % 2, index // 2 % 2, index % 2)
            pairs.append((index, device(*move(*at))))
        return lambda array: lax.ppermute(array, "cache", pairs)

    next_plane = hop(lambda z, y, x, core: ((z + 1) % n_planes, y, x, core))
    first_hop = hop(lambda z, y, x, core: (z, y, 1 - x, core) if core == 0 else (z, 1 - y, x, core))
    second_hop = hop(lambda z, y, x, core: (z, 1 - y, x, core) if core == 0 else (z, y, 1 - x, core))
    other_core = hop(lambda z, y, x, core: (z, y, x, 1 - core))

    me = lax.axis_index("cache")
    z, y, x, core = me // 8, me // 4 % 2, me // 2 % 2, me % 2

    def origin(shift, flip_first, flip_second, side):
        flip_x = jnp.where(side == 0, flip_first, flip_second)
        flip_y = jnp.where(side == 0, flip_second, flip_first)
        return device((z - shift) % n_planes, y ^ flip_y, x ^ flip_x, side)

    def both_cores(shift, *flips):
        return [origin(shift, *flips, side) for side in (core, 1 - core)]

    unused = [0] * 6
    order = both_cores(0, 0, 0) + unused
    for shift in range(n_planes):
        before, after = max(shift - 1, 0), min(shift + 1, n_planes - 1)
        order += both_cores(shift, 1, 0)
        order += [both_cores(shift, 0, 1)[0], both_cores(before, 0, min(shift, 1))[1]]
        order += both_cores(before, 1, 1)
        order += both_cores(after, 0, 0) if after > shift else [both_cores(shift, 0, 1)[1], 0]
    order += both_cores(n_planes - 1, 1, 1) + unused
    order = jnp.stack(order)
    cap = lookup_slot.shape[2]
    cap += -cap % LANES or LANES
    spare = ((0, 0), (0, cap - lookup_slot.shape[2]))
    slots = jnp.pad(lookup_slot[0], spare)[order]
    bag_ids = jnp.pad(lookup_bag[0], spare, constant_values=bags)[order]
    used = jnp.sum((bag_ids < bags).astype(jnp.int32), axis=1)
    steps = (used + UNROLL - 1) // UNROLL
    sum_rows = bags + 8
    places = jnp.where(bag_ids < bags, bag_ids % F * queries + bag_ids // F, bags)
    slots = jnp.where(jnp.arange(cap) == cap - 1, steps[:, None], slots)
    entries = (slots.reshape(-1), places.reshape(-1))

    def of_chip(array):
        return [array, other_core(array)]

    crossed, turned, next_piece = first_hop(own), second_hop(own), next_plane(own)
    sums, done = pool(0, entries, cap, [own], None, sum_rows, [0])
    (crossed,) = gate([crossed], done)
    far, late = [], other_core(own)
    for shift in range(n_planes):
        last = shift == n_planes - 1
        near = of_chip(crossed) + [turned]
        other_turned = other_core(turned)
        next_far = next_plane(far[0]) if shift == n_planes - 2 else second_hop(crossed)
        passed = [next_far]
        if not last:
            passed += [first_hop(next_piece), second_hop(next_piece)]
            piece = of_chip(next_piece)
            if shift < n_planes - 2:
                passed.append(next_plane(next_piece))
        else:
            piece = [other_turned]
        if shift == 0:
            shards, rows = near + [late] + piece, [0, 1, 2, 3, 6, 7]
        else:
            shards, rows = near + [late] + far + piece, list(range(6 + len(piece)))
        sums, done = pool(8 * shift + 8, entries, cap, shards, sums, sum_rows, rows)
        chosen = [0] if last else [1, 0] if shift == n_planes - 2 else [index for index in PICK if index < len(passed)]
        for index, one in zip(chosen, gate([passed[index] for index in chosen], done)):
            passed[index] = one
        next_far, *passed = passed
        far, late = of_chip(next_far), other_turned
        if not last:
            crossed, turned, *next_piece = passed
            next_piece = next_piece[0] if next_piece else None
    args = (8 * n_planes + 8, entries, cap, far, sums, dense_rows)
    if owners == 1:
        return finish(*args, (w_first, w_second, w_out.reshape(1, -1)))
    inter_in = finish(*args, None)[:, : w_first.shape[0]]
    group_inputs = lax.all_gather(inter_in, "owner", axis=0, tiled=True)
    hidden = jax.nn.relu(jnp.dot(group_inputs, w_first, preferred_element_type=jnp.float32))
    second = lax.psum_scatter(
        jnp.dot(hidden.astype(jnp.bfloat16), w_second, preferred_element_type=jnp.float32),
        "owner",
        scatter_dimension=0,
        tiled=True,
    )
    return jnp.sum(jax.nn.relu(second) * w_out, axis=1)


def solution(mesh):
    in_specs = (
        P(("rep", "cache"), None),
        P(("rep", "cache", "owner"), None),
        P(("rep", "cache", "owner"), None),
        P(("rep", "cache"), None),
        P(("rep", "cache", "owner"), None, None),
        P(("rep", "cache", "owner"), None, None),
        P(("rep", "cache", "owner"), None),
        P(None, "owner"),
        P("owner", None),
        P(),
    )
    out_specs = P(("rep", "cache", "owner"))
    return jax.shard_map(
        functools.partial(per_device, mesh.shape["cache"] // 8),
        mesh=mesh,
        in_specs=in_specs,
        out_specs=out_specs,
        check_vma=False,
    )
```

```python
import functools

import jax
import jax.numpy as jnp
from jax import lax
from jax.experimental import pallas as pl
from jax.experimental.pallas import tpu as pltpu
from jax.sharding import PartitionSpec as P

F = 26
BLOCK = 128
VECS = F + 1
LANES = 128
CHAINS = 4
UNROLL = 32
VMEM = 18 << 20
SMEM_SPEC = pl.BlockSpec(memory_space=pltpu.SMEM)
ANY_SPEC = pl.BlockSpec(memory_space=pl.ANY)
HBM_SPEC = pl.BlockSpec(memory_space=pltpu.HBM)
VMEM_SPEC = pl.BlockSpec(memory_space=pltpu.VMEM)


def fill_kernel(slot_ref, block_ref, cache_ref, fills_ref, out_ref, sem):
    def of_block(ref, index):
        return ref.at[pl.ds(pl.multiple_of(index * BLOCK, BLOCK), BLOCK)]

    n_slots = out_ref.shape[0] // BLOCK
    n_fills = slot_ref.shape[0]

    def kept(index):
        hit = slot_ref[0] == index
        for k in range(1, n_fills):
            hit = jnp.logical_or(hit, slot_ref[k] == index)
        return jnp.logical_not(hit)

    def cache_copy(index):
        return pltpu.make_async_copy(of_block(cache_ref, index), of_block(out_ref, index), sem.at[index])

    def fill_copy(k):
        slot = jnp.minimum(slot_ref[k], n_slots - 1)
        return pltpu.make_async_copy(
            of_block(fills_ref, block_ref[k]), of_block(out_ref, slot), sem.at[n_slots + k]
        )

    for k in range(n_fills):
        pl.when(slot_ref[k] < n_slots)(lambda k=k: fill_copy(k).start())
    for index in range(n_slots):
        pl.when(kept(index))(lambda index=index: cache_copy(index).start())
    for index in range(n_slots):
        pl.when(kept(index))(lambda index=index: cache_copy(index).wait())
    for k in range(n_fills):
        pl.when(slot_ref[k] < n_slots)(lambda k=k: fill_copy(k).wait())


def fill(cache_rows, fills, miss_slot, fill_block):
    n_sems = cache_rows.shape[0] // BLOCK + miss_slot.shape[0]
    return pl.pallas_call(
        fill_kernel,
        out_shape=pltpu.VMEM(cache_rows.shape, cache_rows.dtype),
        in_specs=[SMEM_SPEC] * 2 + [ANY_SPEC] * 2,
        out_specs=VMEM_SPEC,
        scratch_shapes=[pltpu.SemaphoreType.DMA((n_sems,))],
        name="fill",
    )(miss_slot, fill_block, cache_rows, fills)


PICK = [1]


def gate_kernel(*refs):
    pass


def gate(arrays, after):
    n_arrays = len(arrays)
    if not arrays:
        return []
    return pl.pallas_call(
        gate_kernel,
        out_shape=[jax.ShapeDtypeStruct(one.shape, one.dtype) for one in arrays],
        in_specs=[ANY_SPEC] * (n_arrays + 1),
        out_specs=[ANY_SPEC] * n_arrays,
        input_output_aliases={index: index for index in range(n_arrays)},
        compiler_params=pltpu.CompilerParams(vmem_limit_bytes=1 << 20),
        name="gate",
    )(*arrays, after)


def pool_shards(first, rows, entry_refs, entry_held, shards, sems, held, table, sums):
    cap = entry_held[0].shape[0] // 8
    copies = [
        pltpu.make_async_copy(ref.at[pl.ds(first * cap, 8 * cap)], to, sems.at[len(shards) + index])
        for index, (ref, to) in enumerate(zip(entry_refs, entry_held))
    ]
    copies += [pltpu.make_async_copy(ref, held.at[s], sems.at[s]) for s, ref in enumerate(shards)]
    for copy in copies:
        copy.start()
    yield
    for copy in copies[:2]:
        copy.wait()
    slot_ref, bag_ref = entry_held
    for s, copy in enumerate(copies[2:]):
        copy.wait()
        table[...] = held[s].astype(jnp.float32)
        row = rows[s]

        def add_entries(step, _):
            start = row * cap + step * UNROLL
            for group in range(UNROLL // CHAINS):
                entries = [start + group * CHAINS + k for k in range(CHAINS)]
                slots = [slot_ref[e] for e in entries]
                bags = [bag_ref[e] for e in entries]
                found = [table[pl.ds(slot, 1), :] for slot in slots]
                olds = [sums[k][pl.ds(bags[k], 1), :] for k in range(CHAINS)]
                for k in range(CHAINS):
                    sums[k][pl.ds(bags[k], 1), :] = olds[k] + found[k]
            return 0

        lax.fori_loop(0, slot_ref[row * cap + cap - 1], add_entries, 0)


def pool_kernel(first, rows, is_first, slot_ref, bag_ref, *refs):
    shards, refs = refs[: len(rows)], refs[len(rows) :]
    if not is_first:
        refs = refs[CHAINS:]
    sums, (_, *entry_held, held, table, sems) = refs[:CHAINS], refs[CHAINS:]
    pooling = pool_shards(
        first, rows, (slot_ref, bag_ref), entry_held, shards, sems, held, table, sums
    )
    next(pooling)
    if is_first:
        for one in sums:
            one[...] = jnp.zeros_like(one)
    for _ in pooling:
        pass


def interact(sums, dense_ref, masked, queries):
    lane = lax.broadcasted_iota(jnp.int32, (8, 256), 1)
    row = lax.broadcasted_iota(jnp.int32, (8, 256), 0)
    own_query = (lane & 7) == row

    def sixteen_queries(step, _):
        dense = dense_ref[pl.ds(pl.multiple_of(step * 16, 16), 16), :].astype(jnp.float32)
        halves = []
        for half in range(2):
            query = pl.multiple_of(step * 16 + half * 8, 8)
            vectors = [dense[half * 8 : half * 8 + 8]]
            for feature in range(F):
                rows = pl.ds(pl.multiple_of(feature * queries + query, 8), 8)
                total = sums[0][rows, :]
                for one in sums[1:]:
                    total = total + one[rows, :]
                vectors.append(total)
            vectors += [jnp.zeros((8, LANES), jnp.float32)] * (32 - VECS)
            stacked = jnp.concatenate(vectors, axis=0).astype(jnp.bfloat16)
            halves.append(
                lax.dot_general(
                    stacked[: 8 * F], stacked, (((1,), (1,)), ((), ())), preferred_element_type=jnp.float32
                )
            )
        for i in range(F):
            pair = [
                jnp.where(own_query, products[8 * i : 8 * i + 8, :], 0.0) for products in halves
            ]
            masked[i, pl.ds(pl.multiple_of(step * 16, 16), 16), :] = jnp.concatenate(
                pair, axis=0
            ).astype(jnp.bfloat16)
        return 0

    lax.fori_loop(0, queries // 16, sixteen_queries, 0, unroll=12)


def inter_columns(masked, dense_ref, inter, queries):
    spread = lax.broadcasted_iota(jnp.int32, (256, LANES), 0) // 8
    vector = lax.broadcasted_iota(jnp.int32, (256, LANES), 1)
    pick = jnp.where(spread == vector, 1.0, 0.0).astype(jnp.bfloat16)
    lane = lax.broadcasted_iota(jnp.int32, (queries, LANES), 1)
    tiles = [jnp.zeros((queries, LANES), jnp.float32) for _ in range(3)]
    first = 0
    for i in range(F):
        length = F - i
        picked = jnp.dot(masked[i], pick, preferred_element_type=jnp.float32)
        shift = (first - (i + 1)) % LANES
        if shift:
            picked = pltpu.roll(picked, shift, 1)
        for tile in range(3):
            low, high = max(first, tile * LANES), min(first + length, (tile + 1) * LANES)
            if low < high:
                inside = jnp.logical_and(lane >= low - tile * LANES, lane < high - tile * LANES)
                tiles[tile] = jnp.where(inside, picked, tiles[tile])
        first += length
    inter[:, :LANES] = dense_ref[...]
    for tile in range(3):
        inter[:, (tile + 1) * LANES : (tile + 2) * LANES] = tiles[tile].astype(jnp.bfloat16)


def final_kernel(first, n_shards, with_head, slot_ref, bag_ref, *refs):
    shards, refs = refs[:n_shards], refs[n_shards:]
    old_sums, dense_ref, refs = refs[:CHAINS], refs[CHAINS], refs[CHAINS + 1 :]
    if with_head:
        w_first, w_second, w_out, logits, *refs = refs
    else:
        inter, *refs = refs
    refs = refs[CHAINS:]
    if with_head:
        inter, first_held, second_held, out_held, weight_sems, *refs = refs
    masked, dense_held, dense_sem, *entry_held, held, table, sems = refs
    queries = dense_ref.shape[0]
    pooling = pool_shards(
        first, (0, 1), (slot_ref, bag_ref), entry_held, shards, sems, held, table, old_sums
    )
    next(pooling)
    dense_copy = pltpu.make_async_copy(dense_ref, dense_held, dense_sem)
    dense_copy.start()
    if with_head:
        weights = [
            pltpu.make_async_copy(w_first, first_held, weight_sems.at[0]),
            pltpu.make_async_copy(w_second, second_held, weight_sems.at[1]),
            pltpu.make_async_copy(w_out, out_held, weight_sems.at[2]),
        ]
        for copy in weights:
            copy.start()
    for _ in pooling:
        pass
    dense_copy.wait()
    interact(old_sums, dense_held, masked, queries)
    inter_columns(masked, dense_held, inter, queries)
    if not with_head:
        return
    for copy in weights:
        copy.wait()
    step = LANES
    inputs = first_held.shape[0]
    for part in range(queries // step):
        rows = slice(part * step, (part + 1) * step)
        hidden = jnp.dot(inter[rows, :inputs], first_held[...], preferred_element_type=jnp.float32)
        hidden = jnp.maximum(hidden, 0.0).astype(jnp.bfloat16)
        second = jnp.dot(hidden, second_held[...], preferred_element_type=jnp.float32)
        scored = jnp.maximum(second, 0.0) * out_held[...]
        folded = scored[:, :LANES]
        for tile in range(1, scored.shape[1] // LANES):
            folded = folded + scored[:, tile * LANES : (tile + 1) * LANES]
        logits[rows] = jnp.sum(folded.T, axis=0)


def pool_scratch(n_shards, shard_rows, cap):
    return [
        pltpu.SMEM((8 * cap,), jnp.int32),
        pltpu.SMEM((8 * cap,), jnp.int32),
        pltpu.VMEM((n_shards, shard_rows, LANES), jnp.bfloat16),
        pltpu.VMEM((shard_rows, LANES), jnp.float32),
        pltpu.SemaphoreType.DMA((n_shards + 2,)),
    ]


def pool(first, entries, cap, shards, sums, sum_rows, rows=(0, 1)):
    n_shards = len(shards)
    is_first = sums is None
    sums = [] if is_first else sums
    *sums, done = pl.pallas_call(
        functools.partial(pool_kernel, first, rows, is_first),
        out_shape=[pltpu.VMEM((sum_rows, LANES), jnp.float32)] * CHAINS
        + [jax.ShapeDtypeStruct((8, LANES), jnp.int32)],
        in_specs=[HBM_SPEC] * 2 + [ANY_SPEC] * n_shards + [VMEM_SPEC] * len(sums),
        out_specs=[VMEM_SPEC] * CHAINS + [ANY_SPEC],
        input_output_aliases={2 + n_shards + k: k for k in range(len(sums))},
        scratch_shapes=pool_scratch(n_shards, shards[0].shape[0], cap),
        compiler_params=pltpu.CompilerParams(vmem_limit_bytes=VMEM),
        cost_estimate=pl.CostEstimate(flops=0, bytes_accessed=n_shards * 3000000, transcendentals=0),
        name="pool",
    )(*entries, *shards, *sums)
    return sums, done


def finish(first, entries, cap, shards, sums, dense_rows, head):
    n_shards = len(shards)
    queries = dense_rows.shape[0]
    width = 4 * LANES
    masked = [
        pltpu.VMEM((F, queries, 256), jnp.bfloat16),
        pltpu.VMEM(dense_rows.shape, dense_rows.dtype),
        pltpu.SemaphoreType.DMA,
    ]
    if head is None:
        head_args, head_specs = [], []
        out_shape = jax.ShapeDtypeStruct((queries, width), jnp.bfloat16)
        scratch = masked
    else:
        head_args, head_specs = list(head), [HBM_SPEC, HBM_SPEC, ANY_SPEC]
        out_shape = jax.ShapeDtypeStruct((queries,), jnp.float32)
        scratch = [
            pltpu.VMEM((queries, width), jnp.bfloat16),
            pltpu.VMEM(head[0].shape, jnp.bfloat16),
            pltpu.VMEM(head[1].shape, jnp.bfloat16),
            pltpu.VMEM(head[2].shape, jnp.float32),
            pltpu.SemaphoreType.DMA((3,)),
            *masked,
        ]
    out = pl.pallas_call(
        functools.partial(final_kernel, first, n_shards, head is not None),
        out_shape=[out_shape] + [pltpu.VMEM(one.shape, one.dtype) for one in sums],
        in_specs=[HBM_SPEC] * 2 + [ANY_SPEC] * n_shards + [VMEM_SPEC] * CHAINS + [ANY_SPEC] + head_specs,
        out_specs=[VMEM_SPEC] * (CHAINS + 1),
        input_output_aliases={2 + n_shards + k: 1 + k for k in range(CHAINS)},
        scratch_shapes=scratch + pool_scratch(n_shards, shards[0].shape[0], cap),
        compiler_params=pltpu.CompilerParams(vmem_limit_bytes=VMEM),
        name="finish",
    )(*entries, *shards, *sums, dense_rows, *head_args)
    return out[0]


def per_device(
    n_planes,
    cache_rows,
    store_rows,
    miss_block,
    miss_slot,
    lookup_slot,
    lookup_bag,
    dense_rows,
    w_first,
    w_second,
    w_out,
):
    emb_width = cache_rows.shape[1]
    queries = dense_rows.shape[0]
    bags = queries * F
    owners = lax.axis_size("owner")
    n_shards = n_planes * 8

    if owners == 1:
        fills, fill_block = store_rows, miss_block[0]
    else:
        fills = store_rows.reshape(-1, BLOCK, emb_width)[miss_block[0]]
        fills = lax.all_gather(fills, "owner", axis=0, tiled=True)
        fill_block = jnp.arange(fills.shape[0], dtype=jnp.int32)
        fills = fills.reshape(-1, emb_width)
    own = fill(cache_rows, fills, miss_slot[0], fill_block)

    def device(z, y, x, core):
        return ((z * 2 + y) * 2 + x) * 2 + core

    def hop(move):
        pairs = []
        for index in range(n_shards):
            at = (index // 8, index // 4 % 2, index // 2 % 2, index % 2)
            pairs.append((index, device(*move(*at))))
        return lambda array: lax.ppermute(array, "cache", pairs)

    next_plane = hop(lambda z, y, x, core: ((z + 1) % n_planes, y, x, core))
    first_hop = hop(lambda z, y, x, core: (z, y, 1 - x, core) if core == 0 else (z, 1 - y, x, core))
    second_hop = hop(lambda z, y, x, core: (z, 1 - y, x, core) if core == 0 else (z, y, 1 - x, core))
    other_core = hop(lambda z, y, x, core: (z, y, x, 1 - core))

    me = lax.axis_index("cache")
    z, y, x, core = me // 8, me // 4 % 2, me // 2 % 2, me % 2

    def origin(shift, flip_first, flip_second, side):
        flip_x = jnp.where(side == 0, flip_first, flip_second)
        flip_y = jnp.where(side == 0, flip_second, flip_first)
        return device((z - shift) % n_planes, y ^ flip_y, x ^ flip_x, side)

    def both_cores(shift, *flips):
        return [origin(shift, *flips, side) for side in (core, 1 - core)]

    unused = [0] * 6
    order = both_cores(0, 0, 0) + unused
    for shift in range(n_planes):
        before, after = max(shift - 1, 0), min(shift + 1, n_planes - 1)
        order += both_cores(shift, 1, 0)
        order += [both_cores(shift, 0, 1)[0], both_cores(before, 0, min(shift, 1))[1]]
        order += both_cores(before, 1, 1)
        order += both_cores(after, 0, 0) if after > shift else [both_cores(shift, 0, 1)[1], 0]
    order += both_cores(n_planes - 1, 1, 1) + unused
    order = jnp.stack(order)
    cap = lookup_slot.shape[2]
    cap += -cap % LANES or LANES
    spare = ((0, 0), (0, cap - lookup_slot.shape[2]))
    slots = jnp.pad(lookup_slot[0], spare)[order]
    bag_ids = jnp.pad(lookup_bag[0], spare, constant_values=bags)[order]
    used = jnp.sum((bag_ids < bags).astype(jnp.int32), axis=1)
    steps = (used + UNROLL - 1) // UNROLL
    sum_rows = bags + 8
    places = jnp.where(bag_ids < bags, bag_ids % F * queries + bag_ids // F, bags)
    slots = jnp.where(jnp.arange(cap) == cap - 1, steps[:, None], slots)
    entries = (slots.reshape(-1), places.reshape(-1))

    def of_chip(array):
        return [array, other_core(array)]

    crossed, turned, next_piece = first_hop(own), second_hop(own), next_plane(own)
    sums, done = pool(0, entries, cap, [own], None, sum_rows, [0])
    (crossed,) = gate([crossed], done)
    far, late = [], [other_core(own)]
    for shift in range(n_planes):
        last = shift == n_planes - 1
        near = of_chip(crossed) + [turned]
        other_turned = other_core(turned)
        next_far = next_plane(far[0]) if shift == n_planes - 2 else second_hop(crossed)
        passed = [next_far]
        if not last:
            passed += [first_hop(next_piece), second_hop(next_piece)]
            piece = of_chip(next_piece)
            if shift < n_planes - 2:
                passed.append(next_plane(next_piece))
        else:
            piece = [other_turned]
        shards = near + late + far + piece
        rows = [0, 1, 2] + [3][: len(late)] + [4, 5][: len(far)] + [6, 7][: len(piece)]
        sums, done = pool(8 * shift + 8, entries, cap, shards, sums, sum_rows, rows)
        if shift == n_planes - 2:
            sums, done = pool(8 * shift + 16, entries, cap, [other_turned], sums, sum_rows, [3])
        chosen = [0] if last else [1, 0] if shift == n_planes - 2 else [index for index in PICK if index < len(passed)]
        for index, one in zip(chosen, gate([passed[index] for index in chosen], done)):
            passed[index] = one
        next_far, *passed = passed
        far, late = of_chip(next_far), [other_turned]
        if shift == n_planes - 2:
            late = []
        if not last:
            crossed, turned, *next_piece = passed
            next_piece = next_piece[0] if next_piece else None
    args = (8 * n_planes + 8, entries, cap, far, sums, dense_rows)
    if owners == 1:
        return finish(*args, (w_first, w_second, w_out.reshape(1, -1)))
    inter_in = finish(*args, None)[:, : w_first.shape[0]]
    group_inputs = lax.all_gather(inter_in, "owner", axis=0, tiled=True)
    hidden = jax.nn.relu(jnp.dot(group_inputs, w_first, preferred_element_type=jnp.float32))
    second = lax.psum_scatter(
        jnp.dot(hidden.astype(jnp.bfloat16), w_second, preferred_element_type=jnp.float32),
        "owner",
        scatter_dimension=0,
        tiled=True,
    )
    return jnp.sum(jax.nn.relu(second) * w_out, axis=1)


def solution(mesh):
    in_specs = (
        P(("rep", "cache"), None),
        P(("rep", "cache", "owner"), None),
        P(("rep", "cache", "owner"), None),
        P(("rep", "cache"), None),
        P(("rep", "cache", "owner"), None, None),
        P(("rep", "cache", "owner"), None, None),
        P(("rep", "cache", "owner"), None),
        P(None, "owner"),
        P("owner", None),
        P(),
    )
    out_specs = P(("rep", "cache", "owner"))
    return jax.shard_map(
        functools.partial(per_device, mesh.shape["cache"] // 8),
        mesh=mesh,
        in_specs=in_specs,
        out_specs=out_specs,
        check_vma=False,
    )
```

```python
import functools

import jax
import jax.numpy as jnp
from jax import lax
from jax.experimental import pallas as pl
from jax.experimental.pallas import tpu as pltpu
from jax.sharding import PartitionSpec as P

F = 26
BLOCK = 128
VECS = F + 1
LANES = 128
CHAINS = 4
UNROLL = 32
VMEM = 18 << 20
SMEM_SPEC = pl.BlockSpec(memory_space=pltpu.SMEM)
ANY_SPEC = pl.BlockSpec(memory_space=pl.ANY)
HBM_SPEC = pl.BlockSpec(memory_space=pltpu.HBM)
VMEM_SPEC = pl.BlockSpec(memory_space=pltpu.VMEM)


def fill_kernel(slot_ref, block_ref, cache_ref, fills_ref, out_ref, sem):
    def of_block(ref, index):
        return ref.at[pl.ds(pl.multiple_of(index * BLOCK, BLOCK), BLOCK)]

    n_slots = out_ref.shape[0] // BLOCK
    n_fills = slot_ref.shape[0]

    def kept(index):
        hit = slot_ref[0] == index
        for k in range(1, n_fills):
            hit = jnp.logical_or(hit, slot_ref[k] == index)
        return jnp.logical_not(hit)

    def cache_copy(index):
        return pltpu.make_async_copy(of_block(cache_ref, index), of_block(out_ref, index), sem.at[index])

    def fill_copy(k):
        slot = jnp.minimum(slot_ref[k], n_slots - 1)
        return pltpu.make_async_copy(
            of_block(fills_ref, block_ref[k]), of_block(out_ref, slot), sem.at[n_slots + k]
        )

    for k in range(n_fills):
        pl.when(slot_ref[k] < n_slots)(lambda k=k: fill_copy(k).start())
    for index in range(n_slots):
        pl.when(kept(index))(lambda index=index: cache_copy(index).start())
    for index in range(n_slots):
        pl.when(kept(index))(lambda index=index: cache_copy(index).wait())
    for k in range(n_fills):
        pl.when(slot_ref[k] < n_slots)(lambda k=k: fill_copy(k).wait())


def fill(cache_rows, fills, miss_slot, fill_block):
    n_sems = cache_rows.shape[0] // BLOCK + miss_slot.shape[0]
    return pl.pallas_call(
        fill_kernel,
        out_shape=pltpu.VMEM(cache_rows.shape, cache_rows.dtype),
        in_specs=[SMEM_SPEC] * 2 + [ANY_SPEC] * 2,
        out_specs=VMEM_SPEC,
        scratch_shapes=[pltpu.SemaphoreType.DMA((n_sems,))],
        name="fill",
    )(miss_slot, fill_block, cache_rows, fills)


PICK = [1]


def gate_kernel(*refs):
    pass


def gate(arrays, after):
    n_arrays = len(arrays)
    if not arrays:
        return []
    return pl.pallas_call(
        gate_kernel,
        out_shape=[jax.ShapeDtypeStruct(one.shape, one.dtype) for one in arrays],
        in_specs=[ANY_SPEC] * (n_arrays + 1),
        out_specs=[ANY_SPEC] * n_arrays,
        input_output_aliases={index: index for index in range(n_arrays)},
        compiler_params=pltpu.CompilerParams(vmem_limit_bytes=1 << 20),
        name="gate",
    )(*arrays, after)


def pool_shards(first, rows, entry_refs, entry_held, shards, sems, held, table, sums):
    cap = entry_held[0].shape[0] // 8
    copies = [
        pltpu.make_async_copy(ref.at[pl.ds(first * cap, 8 * cap)], to, sems.at[len(shards) + index])
        for index, (ref, to) in enumerate(zip(entry_refs, entry_held))
    ]
    copies += [pltpu.make_async_copy(ref, held.at[s], sems.at[s]) for s, ref in enumerate(shards)]
    for copy in copies:
        copy.start()
    yield
    for copy in copies[:2]:
        copy.wait()
    slot_ref, bag_ref = entry_held
    for s, copy in enumerate(copies[2:]):
        copy.wait()
        table[...] = held[s].astype(jnp.float32)
        row = rows[s]

        def add_entries(step, _):
            start = row * cap + step * UNROLL
            for group in range(UNROLL // CHAINS):
                entries = [start + group * CHAINS + k for k in range(CHAINS)]
                slots = [slot_ref[e] for e in entries]
                bags = [bag_ref[e] for e in entries]
                found = [table[pl.ds(slot, 1), :] for slot in slots]
                olds = [sums[k][pl.ds(bags[k], 1), :] for k in range(CHAINS)]
                for k in range(CHAINS):
                    sums[k][pl.ds(bags[k], 1), :] = olds[k] + found[k]
            return 0

        lax.fori_loop(0, slot_ref[row * cap + cap - 1], add_entries, 0)


def pool_kernel(first, rows, is_first, slot_ref, bag_ref, *refs):
    shards, refs = refs[: len(rows)], refs[len(rows) :]
    if not is_first:
        refs = refs[CHAINS:]
    sums, (_, *entry_held, held, table, sems) = refs[:CHAINS], refs[CHAINS:]
    pooling = pool_shards(
        first, rows, (slot_ref, bag_ref), entry_held, shards, sems, held, table, sums
    )
    next(pooling)
    if is_first:
        for one in sums:
            one[...] = jnp.zeros_like(one)
    for _ in pooling:
        pass


def first_lane(i):
    return 8 * (i + 1) // LANES * LANES


def interact(sums, dense_ref, masked, queries):
    own_query = {
        low: (lax.broadcasted_iota(jnp.int32, (8, 256 - low), 1) & 7)
        == lax.broadcasted_iota(jnp.int32, (8, 256 - low), 0)
        for low in (0, LANES)
    }

    def sixteen_queries(step, _):
        dense = dense_ref[pl.ds(pl.multiple_of(step * 16, 16), 16), :].astype(jnp.float32)
        halves = []
        for half in range(2):
            query = pl.multiple_of(step * 16 + half * 8, 8)
            vectors = [dense[half * 8 : half * 8 + 8]]
            for feature in range(F):
                rows = pl.ds(pl.multiple_of(feature * queries + query, 8), 8)
                total = sums[0][rows, :]
                for one in sums[1:]:
                    total = total + one[rows, :]
                vectors.append(total)
            vectors += [jnp.zeros((8, LANES), jnp.float32)] * (32 - VECS)
            stacked = jnp.concatenate(vectors, axis=0).astype(jnp.bfloat16)
            halves.append(
                lax.dot_general(
                    stacked[: 8 * F], stacked, (((1,), (1,)), ((), ())), preferred_element_type=jnp.float32
                )
            )
        for i in range(F):
            low = first_lane(i)
            pair = [
                jnp.where(own_query[low], products[8 * i : 8 * i + 8, low:], 0.0) for products in halves
            ]
            masked[i, pl.ds(pl.multiple_of(step * 16, 16), 16), low:] = jnp.concatenate(
                pair, axis=0
            ).astype(jnp.bfloat16)
        return 0

    lax.fori_loop(0, queries // 16, sixteen_queries, 0, unroll=12)


def inter_columns(masked, dense_ref, inter, queries):
    spread = lax.broadcasted_iota(jnp.int32, (256, LANES), 0) // 8
    vector = lax.broadcasted_iota(jnp.int32, (256, LANES), 1)
    pick = jnp.where(spread == vector, 1.0, 0.0).astype(jnp.bfloat16)
    lane = lax.broadcasted_iota(jnp.int32, (queries, LANES), 1)
    tiles = [jnp.zeros((queries, LANES), jnp.float32) for _ in range(3)]
    first = 0
    for i in range(F):
        length = F - i
        low = first_lane(i)
        picked = jnp.dot(masked[i, :, low:], pick[low:], preferred_element_type=jnp.float32)
        shift = (first - (i + 1)) % LANES
        if shift:
            picked = pltpu.roll(picked, shift, 1)
        for tile in range(3):
            low, high = max(first, tile * LANES), min(first + length, (tile + 1) * LANES)
            if low < high:
                inside = jnp.logical_and(lane >= low - tile * LANES, lane < high - tile * LANES)
                tiles[tile] = jnp.where(inside, picked, tiles[tile])
        first += length
    inter[:, :LANES] = dense_ref[...]
    for tile in range(3):
        inter[:, (tile + 1) * LANES : (tile + 2) * LANES] = tiles[tile].astype(jnp.bfloat16)


def final_kernel(first, n_shards, with_head, slot_ref, bag_ref, *refs):
    shards, refs = refs[:n_shards], refs[n_shards:]
    old_sums, dense_ref, refs = refs[:CHAINS], refs[CHAINS], refs[CHAINS + 1 :]
    if with_head:
        w_first, w_second, w_out, logits, *refs = refs
    else:
        inter, *refs = refs
    refs = refs[CHAINS:]
    if with_head:
        inter, first_held, second_held, out_held, weight_sems, *refs = refs
    masked, dense_held, dense_sem, *entry_held, held, table, sems = refs
    queries = dense_ref.shape[0]
    pooling = pool_shards(
        first, (0, 1), (slot_ref, bag_ref), entry_held, shards, sems, held, table, old_sums
    )
    next(pooling)
    dense_copy = pltpu.make_async_copy(dense_ref, dense_held, dense_sem)
    dense_copy.start()
    if with_head:
        weights = [
            pltpu.make_async_copy(w_first, first_held, weight_sems.at[0]),
            pltpu.make_async_copy(w_second, second_held, weight_sems.at[1]),
            pltpu.make_async_copy(w_out, out_held, weight_sems.at[2]),
        ]
        for copy in weights:
            copy.start()
    for _ in pooling:
        pass
    dense_copy.wait()
    interact(old_sums, dense_held, masked, queries)
    inter_columns(masked, dense_held, inter, queries)
    if not with_head:
        return
    for copy in weights:
        copy.wait()
    step = LANES
    inputs = first_held.shape[0]
    for part in range(queries // step):
        rows = slice(part * step, (part + 1) * step)
        hidden = jnp.dot(inter[rows, :inputs], first_held[...], preferred_element_type=jnp.float32)
        hidden = jnp.maximum(hidden, 0.0).astype(jnp.bfloat16)
        second = jnp.dot(hidden, second_held[...], preferred_element_type=jnp.float32)
        scored = jnp.maximum(second, 0.0) * out_held[...]
        folded = scored[:, :LANES]
        for tile in range(1, scored.shape[1] // LANES):
            folded = folded + scored[:, tile * LANES : (tile + 1) * LANES]
        logits[rows] = jnp.sum(folded.T, axis=0)


def pool_scratch(n_shards, shard_rows, cap):
    return [
        pltpu.SMEM((8 * cap,), jnp.int32),
        pltpu.SMEM((8 * cap,), jnp.int32),
        pltpu.VMEM((n_shards, shard_rows, LANES), jnp.bfloat16),
        pltpu.VMEM((shard_rows, LANES), jnp.float32),
        pltpu.SemaphoreType.DMA((n_shards + 2,)),
    ]


def pool(first, entries, cap, shards, sums, sum_rows, rows=(0, 1)):
    n_shards = len(shards)
    is_first = sums is None
    sums = [] if is_first else sums
    *sums, done = pl.pallas_call(
        functools.partial(pool_kernel, first, rows, is_first),
        out_shape=[pltpu.VMEM((sum_rows, LANES), jnp.float32)] * CHAINS
        + [jax.ShapeDtypeStruct((8, LANES), jnp.int32)],
        in_specs=[HBM_SPEC] * 2 + [ANY_SPEC] * n_shards + [VMEM_SPEC] * len(sums),
        out_specs=[VMEM_SPEC] * CHAINS + [ANY_SPEC],
        input_output_aliases={2 + n_shards + k: k for k in range(len(sums))},
        scratch_shapes=pool_scratch(n_shards, shards[0].shape[0], cap),
        compiler_params=pltpu.CompilerParams(vmem_limit_bytes=VMEM),
        cost_estimate=pl.CostEstimate(flops=0, bytes_accessed=n_shards * 3000000, transcendentals=0),
        name="pool",
    )(*entries, *shards, *sums)
    return sums, done


def finish(first, entries, cap, shards, sums, dense_rows, head):
    n_shards = len(shards)
    queries = dense_rows.shape[0]
    width = 4 * LANES
    masked = [
        pltpu.VMEM((F, queries, 256), jnp.bfloat16),
        pltpu.VMEM(dense_rows.shape, dense_rows.dtype),
        pltpu.SemaphoreType.DMA,
    ]
    if head is None:
        head_args, head_specs = [], []
        out_shape = jax.ShapeDtypeStruct((queries, width), jnp.bfloat16)
        scratch = masked
    else:
        head_args, head_specs = list(head), [HBM_SPEC, HBM_SPEC, ANY_SPEC]
        out_shape = jax.ShapeDtypeStruct((queries,), jnp.float32)
        scratch = [
            pltpu.VMEM((queries, width), jnp.bfloat16),
            pltpu.VMEM(head[0].shape, jnp.bfloat16),
            pltpu.VMEM(head[1].shape, jnp.bfloat16),
            pltpu.VMEM(head[2].shape, jnp.float32),
            pltpu.SemaphoreType.DMA((3,)),
            *masked,
        ]
    out = pl.pallas_call(
        functools.partial(final_kernel, first, n_shards, head is not None),
        out_shape=[out_shape] + [pltpu.VMEM(one.shape, one.dtype) for one in sums],
        in_specs=[HBM_SPEC] * 2 + [ANY_SPEC] * n_shards + [VMEM_SPEC] * CHAINS + [ANY_SPEC] + head_specs,
        out_specs=[VMEM_SPEC] * (CHAINS + 1),
        input_output_aliases={2 + n_shards + k: 1 + k for k in range(CHAINS)},
        scratch_shapes=scratch + pool_scratch(n_shards, shards[0].shape[0], cap),
        compiler_params=pltpu.CompilerParams(vmem_limit_bytes=VMEM),
        name="finish",
    )(*entries, *shards, *sums, dense_rows, *head_args)
    return out[0]


def per_device(
    n_planes,
    cache_rows,
    store_rows,
    miss_block,
    miss_slot,
    lookup_slot,
    lookup_bag,
    dense_rows,
    w_first,
    w_second,
    w_out,
):
    emb_width = cache_rows.shape[1]
    queries = dense_rows.shape[0]
    bags = queries * F
    owners = lax.axis_size("owner")
    n_shards = n_planes * 8

    if owners == 1:
        fills, fill_block = store_rows, miss_block[0]
    else:
        fills = store_rows.reshape(-1, BLOCK, emb_width)[miss_block[0]]
        fills = lax.all_gather(fills, "owner", axis=0, tiled=True)
        fill_block = jnp.arange(fills.shape[0], dtype=jnp.int32)
        fills = fills.reshape(-1, emb_width)
    own = fill(cache_rows, fills, miss_slot[0], fill_block)

    def device(z, y, x, core):
        return ((z * 2 + y) * 2 + x) * 2 + core

    def hop(move):
        pairs = []
        for index in range(n_shards):
            at = (index // 8, index // 4 % 2, index // 2 % 2, index % 2)
            pairs.append((index, device(*move(*at))))
        return lambda array: lax.ppermute(array, "cache", pairs)

    next_plane = hop(lambda z, y, x, core: ((z + 1) % n_planes, y, x, core))
    first_hop = hop(lambda z, y, x, core: (z, y, 1 - x, core) if core == 0 else (z, 1 - y, x, core))
    second_hop = hop(lambda z, y, x, core: (z, 1 - y, x, core) if core == 0 else (z, y, 1 - x, core))
    other_core = hop(lambda z, y, x, core: (z, y, x, 1 - core))

    me = lax.axis_index("cache")
    z, y, x, core = me // 8, me // 4 % 2, me // 2 % 2, me % 2

    def origin(shift, flip_first, flip_second, side):
        flip_x = jnp.where(side == 0, flip_first, flip_second)
        flip_y = jnp.where(side == 0, flip_second, flip_first)
        return device((z - shift) % n_planes, y ^ flip_y, x ^ flip_x, side)

    def both_cores(shift, *flips):
        return [origin(shift, *flips, side) for side in (core, 1 - core)]

    unused = [0] * 6
    order = both_cores(0, 0, 0) + unused
    for shift in range(n_planes):
        before, after = max(shift - 1, 0), min(shift + 1, n_planes - 1)
        order += both_cores(shift, 1, 0)
        order += [both_cores(shift, 0, 1)[0], both_cores(before, 0, min(shift, 1))[1]]
        order += both_cores(before, 1, 1)
        order += both_cores(after, 0, 0) if after > shift else [both_cores(shift, 0, 1)[1], 0]
    order += both_cores(n_planes - 1, 1, 1) + unused
    order = jnp.stack(order)
    cap = lookup_slot.shape[2]
    cap += -cap % LANES or LANES
    spare = ((0, 0), (0, cap - lookup_slot.shape[2]))
    slots = jnp.pad(lookup_slot[0], spare)[order]
    bag_ids = jnp.pad(lookup_bag[0], spare, constant_values=bags)[order]
    used = jnp.sum((bag_ids < bags).astype(jnp.int32), axis=1)
    steps = (used + UNROLL - 1) // UNROLL
    sum_rows = bags + 8
    places = jnp.where(bag_ids < bags, bag_ids % F * queries + bag_ids // F, bags)
    slots = jnp.where(jnp.arange(cap) == cap - 1, steps[:, None], slots)
    entries = (slots.reshape(-1), places.reshape(-1))

    def of_chip(array):
        return [array, other_core(array)]

    crossed, turned, next_piece = first_hop(own), second_hop(own), next_plane(own)
    sums, done = pool(0, entries, cap, [own], None, sum_rows, [0])
    (crossed,) = gate([crossed], done)
    far, late = [], [other_core(own)]
    for shift in range(n_planes):
        last = shift == n_planes - 1
        near = of_chip(crossed) + [turned]
        other_turned = other_core(turned)
        next_far = next_plane(far[0]) if shift == n_planes - 2 else second_hop(crossed)
        passed = [next_far]
        if not last:
            passed += [first_hop(next_piece), second_hop(next_piece)]
            piece = of_chip(next_piece)
            if shift < n_planes - 2:
                passed.append(next_plane(next_piece))
        else:
            piece = [other_turned]
        shards = near + late + far + piece
        rows = [0, 1, 2] + [3][: len(late)] + [4, 5][: len(far)] + [6, 7][: len(piece)]
        sums, done = pool(8 * shift + 8, entries, cap, shards, sums, sum_rows, rows)
        if shift == n_planes - 2:
            sums, done = pool(8 * shift + 16, entries, cap, [other_turned], sums, sum_rows, [3])
        chosen = [0] if last else [1, 0] if shift == n_planes - 2 else [index for index in PICK if index < len(passed)]
        for index, one in zip(chosen, gate([passed[index] for index in chosen], done)):
            passed[index] = one
        next_far, *passed = passed
        far, late = of_chip(next_far), [other_turned]
        if shift == n_planes - 2:
            late = []
        if not last:
            crossed, turned, *next_piece = passed
            next_piece = next_piece[0] if next_piece else None
    args = (8 * n_planes + 8, entries, cap, far, sums, dense_rows)
    if owners == 1:
        return finish(*args, (w_first, w_second, w_out.reshape(1, -1)))
    inter_in = finish(*args, None)[:, : w_first.shape[0]]
    group_inputs = lax.all_gather(inter_in, "owner", axis=0, tiled=True)
    hidden = jax.nn.relu(jnp.dot(group_inputs, w_first, preferred_element_type=jnp.float32))
    second = lax.psum_scatter(
        jnp.dot(hidden.astype(jnp.bfloat16), w_second, preferred_element_type=jnp.float32),
        "owner",
        scatter_dimension=0,
        tiled=True,
    )
    return jnp.sum(jax.nn.relu(second) * w_out, axis=1)


def solution(mesh):
    in_specs = (
        P(("rep", "cache"), None),
        P(("rep", "cache", "owner"), None),
        P(("rep", "cache", "owner"), None),
        P(("rep", "cache"), None),
        P(("rep", "cache", "owner"), None, None),
        P(("rep", "cache", "owner"), None, None),
        P(("rep", "cache", "owner"), None),
        P(None, "owner"),
        P("owner", None),
        P(),
    )
    out_specs = P(("rep", "cache", "owner"))
    return jax.shard_map(
        functools.partial(per_device, mesh.shape["cache"] // 8),
        mesh=mesh,
        in_specs=in_specs,
        out_specs=out_specs,
        check_vma=False,
    )
```
